32 devices in a mesh: dp: 8 (over y, x, core), tensor: 4 (over z).
Axes of the slice: x: 2, y: 2, z: 4, core: 2. Of those that a mesh axis runs over, the one named last changes fastest.
Arguments:
- tokens: bfloat16 [4096, 768], P(('dp', 'tensor')), may hold values from -6 to 6
- gain_attn: float32 [768], replicated, may hold values from 0.5 to 1.5
- gain_ffn: float32 [768], replicated, may hold values from 0.5 to 1.5
- w_query: bfloat16 [768, 768], P('dp', 'tensor'), may hold values from -0.078125 to 0.078125
- w_key: bfloat16 [768, 768], P('dp', 'tensor'), may hold values from -0.21875 to 0.21875
- w_value: bfloat16 [768, 768], P('dp', 'tensor'), may hold values from -0.21875 to 0.21875
- w_output: bfloat16 [768, 768], P('dp', 'tensor'), may hold values from -0.875 to 0.875
- bias_table: float32 [32, 12], replicated, may hold values from -4 to 4
- router: float32 [768, 2], replicated, may hold values from -0.15625 to 0.15625
- w_in: bfloat16 [768, 2, 3072], P('dp', None, 'tensor'), may hold values from -0.21875 to 0.21875
- w_out: bfloat16 [768, 2, 3072], P('dp', None, 'tensor'), may hold values from -0.3125 to 0.3125
- routes: int32 [4096, 1], P('dp'), may hold values from 0 to 1; in each aligned block of 512 rows (0 to 511, 512 to 1023, ...) at most 384 rows name the same one
- lengths: int32 [8, 4], P('dp'), may hold values from 1 to 448, 512 in all within a row
- cotangent: bfloat16 [4096, 768], P(('dp', 'tensor')), may hold values from -6 to 6
Outputs:
- mixed_out: bfloat16 [4096, 768], P(('dp', 'tensor'))
- grad_tokens: float32 [4096, 768], P(('dp', 'tensor'))
- grad_gain_attn: float32 [768], replicated
- grad_gain_ffn: float32 [768], replicated
- grad_query: float32 [768, 768], P('dp', 'tensor')
- grad_key: float32 [768, 768], P('dp', 'tensor')
- grad_value: float32 [768, 768], P('dp', 'tensor')
- grad_output: float32 [768, 768], P('dp', 'tensor')
- grad_bias: float32 [32, 12], replicated
- grad_router: float32 [768, 2], replicated
- grad_in: float32 [768, 2, 3072], P('dp', None, 'tensor')
- grad_out: float32 [768, 2, 3072], P('dp', None, 'tensor')
The draws below stay inside these ranges and needn't reach their ends.
Inputs may be any that keep to these rules, and one draw needn't show every extreme that they name: `routes`: in each group (aligned block of 512 tokens) no expert has more than 384 tokens. Each group's lengths sum to 512, and its longest is exactly 448.
All inputs are finite; a program needn't handle non-finite values.
Results may differ from the reference program's by a relative error of at most 0.017.
Values may be sent and summed in bfloat16 or wider, within the bound.
A program may use at most 128 MiB of HBM per device.

```python
import math
import jax
import jax.numpy as jnp
import numpy as np
from jax import lax

D = 768
HEADS = 12
HEAD_DIM = 64
FF = 3072
EXPERTS = 2
BUCKETS = 32
SEQS = 4
TOK_DEV = 128
GROUPS = 8
TOKENS = 4096
LONGEST = 448
CAP = 384
N_TENSOR = 4


def level_of(rng, dims, pieces, low, top_value):
    def one(axis_at, parts):
        draws = jax.random.uniform(jax.random.fold_in(jax.random.fold_in(rng, 6), axis_at), (parts,), jnp.float32, low / len(pieces), top_value / len(pieces))
        return jnp.repeat(jnp.exp(draws), dims[axis_at] // parts).reshape((-1,) + (1,) * (len(dims) - axis_at - 1))

    factor_of = one(*pieces[0])
    for cut in pieces[1:]:
        factor_of = factor_of * one(*cut)
    return factor_of


def profile(number_of, total, reach, lean):
    weights = [(1 << 20) // math.isqrt(grade ** lean) + 1 for grade in range(2, number_of + 1)]
    rest, given = total - reach - (number_of - 1), [1] * (number_of - 1)
    while rest > 0:
        candidates = [i for i in range(number_of - 1) if given[i] < reach]
        pool, remaining = sum([weights[i] for i in candidates]), rest
        for i in candidates:
            addition = min(reach - given[i], max(1, remaining * weights[i] // pool), rest)
            given[i] = given[i] + addition
            rest = rest - addition
    return np.array([reach] + given)


def uneven_parts(rng, number_of, total, reach, slope):
    if number_of == 2:
        one = jax.random.randint(rng, (), max(1, total - reach), min(reach, total - 1) + 1)
        return jnp.stack([one, total - one])
    sizes = jnp.asarray(profile(number_of, total, reach, slope), jnp.int32)
    couples = (number_of - 1) // 2
    donor, taker = sizes[1:1 + 2 * couples:2], sizes[2:2 + 2 * couples:2]
    margin = jnp.minimum(donor - 1, reach - taker)
    moved = jax.random.randint(jax.random.fold_in(rng, 1), (couples,), 0, 1 << 20) % (margin + 1)
    sizes = sizes.at[1:1 + 2 * couples:2].set(donor - moved).at[2:2 + 2 * couples:2].set(taker + moved)
    return sizes[jax.random.permutation(jax.random.fold_in(rng, 2), number_of)]


def assign_block(key, own, number, rows, count, top, bound, lean):
    sequence = jax.random.permutation(key, count)
    crowded, ordinary = shares(count, rows * top, bound, lean, True), shares(count, rows * top, bound, lean, False)
    places = jnp.arange(count)

    def named(sizes, offset_by):
        used = int((sizes > 0).sum())
        fixed = max(1, used // 4)
        shifted = fixed + (places - fixed + offset_by * (used - fixed)) % max(1, count - fixed)
        return jnp.zeros((count,), jnp.int32).at[sequence[jnp.where(places < fixed, places, shifted)]].set(jnp.asarray(sizes, jnp.int32))

    sizes = jnp.where(number % 4 == 0, named(crowded, number // 4), named(ordinary, number - number // 4 - 1))
    mixed = jax.random.permutation(jax.random.fold_in(own, 3), count)
    source_of, receiver = mixed[0:count // 2 * 2:2], mixed[1:count // 2 * 2:2]
    slack = jnp.minimum(sizes[source_of] - 1, bound - sizes[receiver]) // 2
    slack = jnp.where((source_of == sequence[0]) | (receiver == sequence[0]) | (sizes[receiver] == 0), 0, jnp.maximum(slack, 0))
    shifted = jax.random.randint(jax.random.fold_in(own, 4), (count // 2,), 0, 1 << 20) % (slack + 1)
    sizes = sizes.at[source_of].add(-shifted).at[receiver].add(shifted)
    labels = jnp.searchsorted(jnp.cumsum(sizes), jnp.arange(rows * top), side="right").astype(jnp.int32)
    table = labels.reshape(top, rows).T
    table = table[jax.random.permutation(jax.random.fold_in(own, 1), rows)]
    offset_by = jax.random.randint(jax.random.fold_in(own, 2), (rows, 1), 0, top)
    return jnp.take_along_axis(table, (jnp.arange(top)[None, :] + offset_by) % top, axis=1)


def shares(amount, total, most, skew, full):
    weights = [(1 << 20) // math.isqrt(rank ** skew) + 1 for rank in range(1, amount + 1)]
    largest = most if full else min(most, max(-(-total // amount), total * weights[0] // sum(weights)))
    least = 1 if total - largest >= amount - 1 else 0
    given, rest = [largest] + [least] * (amount - 1), total - largest - least * (amount - 1)
    while rest > 0:
        movable = [i for i in range(1, amount) if given[i] < largest] or [i for i in range(1, amount) if given[i] < most]
        whole, budget = sum([weights[i] for i in movable]), rest
        for i in movable:
            more = min(most - given[i], max(1, budget * weights[i] // whole), rest)
            given[i] = given[i] + more
            rest = rest - more
    return np.array(given)


def normal_values(stream_key, dims, spread, most, cuts=(), kind=jnp.bfloat16):
    level = level_of(stream_key, dims, cuts, -0.22, 0.18) if cuts else 1.0
    array = jax.random.normal(stream_key, dims, jnp.float32) * spread * level
    return jnp.minimum(jnp.maximum(array, -most), most).astype(kind)


def setup_inputs(seed: int = 0) -> dict:
    splits = jax.random.split(jax.random.key(seed), 15)
    tokens = normal_values(splits[0], (TOKENS, D), 1.0, 6.0, ((0, 32),))
    gain_attn = jnp.clip(1.0 + 0.1 * jax.random.normal(splits[1], (D,), jnp.float32), 0.5, 1.5)
    gain_ffn = jnp.clip(1.0 + 0.1 * jax.random.normal(splits[2], (D,), jnp.float32), 0.5, 1.5)
    w_query = normal_values(splits[3], (D, D), (8 * D) ** -0.5, 0.078125, ((0, 8), (1, 4)))
    w_key = normal_values(splits[4], (D, D), D ** -0.5, 0.21875, ((0, 8), (1, 4)))
    w_value = normal_values(splits[5], (D, D), D ** -0.5, 0.21875, ((0, 8), (1, 4)))
    w_output = normal_values(splits[6], (D, D), (D // 16) ** -0.5, 0.875, ((0, 8), (1, 4)))
    bias_table = normal_values(splits[7], (BUCKETS, HEADS), 1.0, 4.0, (), jnp.float32)
    router = normal_values(splits[8], (D, EXPERTS), (2 * D) ** -0.5, 0.15625, (), jnp.float32)
    w_in = normal_values(splits[9], (D, EXPERTS, FF), D ** -0.5, 0.21875, ((0, 8), (2, 4)))
    w_out = normal_values(splits[10], (D, EXPERTS, FF), (FF // 8) ** -0.5, 0.3125, ((0, 8), (2, 4)))
    routes_keys = jax.random.split(jax.random.fold_in(splits[11], 1), TOKENS // (TOK_DEV * N_TENSOR))
    routes_turns = jax.random.permutation(jax.random.fold_in(splits[11], 3), TOKENS // (TOK_DEV * N_TENSOR))
    routes = jax.vmap(lambda own, number: assign_block(jax.random.fold_in(splits[11], 2), own, number, TOK_DEV * N_TENSOR, EXPERTS, 1, CAP, 1))(routes_keys, routes_turns).reshape((TOKENS, 1))
    lengths = jax.vmap(lambda own: uneven_parts(own, SEQS, TOK_DEV * N_TENSOR, LONGEST, 2))(jax.random.split(splits[12], GROUPS)).reshape((GROUPS, SEQS)).astype(jnp.int32)
    cotangent = normal_values(splits[13], (TOKENS, D), 1.0, 6.0, ((0, 32),))
    return dict(tokens=tokens, gain_attn=gain_attn, gain_ffn=gain_ffn, w_query=w_query, w_key=w_key, w_value=w_value, w_output=w_output, bias_table=bias_table, router=router, w_in=w_in, w_out=w_out, routes=routes, lengths=lengths, cotangent=cotangent)


@jax.custom_vjp
def low(v):
    return lax.optimization_barrier(v.astype(jnp.bfloat16)).astype(jnp.float32)

@jax.custom_vjp
def low_back(v):
    return v

def low_keep(v):
    return (low(v), None)

def low_pass(kept, grad):
    return (grad,)

def back_keep(v):
    return (v, None)

def back_low(kept, grad):
    return (low(grad),)
low.defvjp(low_keep, low_pass)
low_back.defvjp(back_keep, back_low)
highest = lax.Precision.HIGHEST
bucket_edges = (12, 16, 23, 32, 46, 64, 91)

def rms_scale(values, gain):
    return values * lax.rsqrt(lax.optimization_barrier(jnp.mean(values * values, axis=-1, keepdims=True)) + 1e-06) * gain

def position_buckets(length):
    position = jnp.arange(length, dtype=jnp.int32)
    relative = position[None, :] - position[:, None]
    distance = jnp.abs(relative)
    far_part = jnp.full(distance.shape, 8, jnp.int32)
    for edge in bucket_edges:
        far_part = far_part + (distance >= edge).astype(jnp.int32)
    return jnp.where(distance < 8, distance, far_part) + 16 * (relative > 0).astype(jnp.int32)

def same_sequence(seq_lengths, length):
    position = jnp.arange(length, dtype=jnp.int32)
    ends = jnp.cumsum(seq_lengths).astype(jnp.int32)
    segment = lax.optimization_barrier(jnp.sum((position[:, None] >= ends[None, :]).astype(jnp.int32), axis=1))
    return segment[:, None] == segment[None, :]

def expert_slots(route_ids, capacity):
    onehot = (route_ids[:, None] == jnp.arange(EXPERTS, dtype=jnp.int32)[None, :]).astype(jnp.int32)
    before = jnp.cumsum(onehot, axis=0) - onehot
    slot_of = lax.optimization_barrier(jnp.sum(before * onehot, axis=1)).astype(jnp.int32)
    counts = lax.optimization_barrier(jnp.sum(onehot, axis=0))
    token_of = jnp.zeros((EXPERTS, capacity), jnp.int32).at[route_ids, slot_of].set(jnp.arange(route_ids.shape[0], dtype=jnp.int32))
    filled = jnp.arange(capacity, dtype=jnp.int32)[None, :] < counts[:, None]
    return (slot_of, token_of, filled)

def group_layer(params, tok_rows, route_ids, seq_lengths):
    gain_attn, gain_ffn, w_query, w_key, w_value, w_output, bias_table, router, w_in, w_out = params
    group_rows = tok_rows.shape[0]
    normed = low(rms_scale(tok_rows, gain_attn))
    query = low(low_back(jnp.dot(normed, w_query, precision=highest)))
    key_proj = low(low_back(jnp.dot(normed, w_key, precision=highest)))
    value_proj = low(low_back(jnp.dot(normed, w_value, precision=highest)))
    same_seq = same_sequence(seq_lengths, group_rows)
    bucket = position_buckets(group_rows)
    biases = jnp.transpose(bias_table[bucket], (2, 0, 1))
    query_heads = query.reshape(group_rows, HEADS, HEAD_DIM)
    key_heads = key_proj.reshape(group_rows, HEADS, HEAD_DIM)
    value_heads = value_proj.reshape(group_rows, HEADS, HEAD_DIM)
    scores = jnp.einsum('qhd,khd->hqk', query_heads, key_heads, precision=highest) + biases
    scores = low_back(scores)
    scores = jnp.where(same_seq[None], scores, -1e+30)
    top = lax.optimization_barrier(jnp.max(scores, axis=-1, keepdims=True))
    weights = jnp.exp(scores - top)
    probs = low(weights / lax.optimization_barrier(jnp.sum(weights, axis=-1, keepdims=True)))
    attended = jnp.einsum('hqk,khd->qhd', probs, value_heads, precision=highest).reshape(group_rows, D)
    attended = low(low_back(attended))
    branch = low_back(jnp.dot(attended, w_output.T, precision=highest))
    middle = tok_rows + branch
    normed_ffn = low(rms_scale(middle, gain_ffn))
    logits = jnp.dot(normed_ffn, router, precision=highest)
    router_probs = jax.nn.softmax(logits, axis=-1)
    onehot = (route_ids[:, None] == jnp.arange(EXPERTS, dtype=jnp.int32)[None, :]).astype(jnp.float32)
    gate = lax.optimization_barrier(jnp.sum(router_probs * onehot, axis=1))
    slot_of, token_of, filled = expert_slots(route_ids, CAP)
    inputs = jnp.where(filled[..., None], normed_ffn[token_of], 0.0)
    pre = low_back(jnp.einsum('ecd,def->ecf', inputs, w_in, precision=highest))
    active = low(jax.nn.gelu(pre, approximate=True))
    expert_out = jnp.einsum('ecf,def->ecd', active, w_out, precision=highest)
    returned = low_back(expert_out[route_ids, slot_of])
    return middle + gate[:, None] * returned

def reference(tokens, gain_attn, gain_ffn, w_query, w_key, w_value, w_output, bias_table, router, w_in, w_out, routes, lengths, cotangent):
    group_rows = TOK_DEV * N_TENSOR
    route_groups = routes.reshape(GROUPS, group_rows).astype(jnp.int32)

    def forward(tok_f32, gain_a, gain_f, wq_f, wk_f, wv_f, wo_f, table_f, router_f, win_f, wout_f):
        params = (gain_a, gain_f, wq_f, wk_f, wv_f, wo_f, table_f, router_f, win_f, wout_f)

        def one_group(item):
            return group_layer(params, item[0], item[1], item[2])
        result = lax.map(jax.checkpoint(one_group), (tok_f32.reshape(GROUPS, group_rows, D), route_groups, lengths))
        return result.reshape(TOKENS, D)
    primal = (tokens.astype(jnp.float32), gain_attn, gain_ffn, w_query.astype(jnp.float32), w_key.astype(jnp.float32), w_value.astype(jnp.float32), w_output.astype(jnp.float32), bias_table, router, w_in.astype(jnp.float32), w_out.astype(jnp.float32))
    result, back_fn = jax.vjp(forward, *primal)
    grads = back_fn(cotangent.astype(jnp.float32))
    return (result.astype(jnp.bfloat16), grads[0], grads[1], grads[2], grads[3], grads[4], grads[5], grads[6], grads[7], grads[8], grads[9], grads[10])
```

```python
import functools

import jax
import jax.numpy as jnp
from jax import lax
from jax.experimental import pallas as pl
from jax.experimental.pallas import tpu as pltpu
from jax.sharding import PartitionSpec as P

HEAD_DIM = 64
EXPERTS = 2
BUCKETS = 32


highest = lax.Precision.HIGHEST
bucket_edges = (12, 16, 23, 32, 46, 64, 91)


def rms_scale(values, gain):
    return values * lax.rsqrt(jnp.mean(values * values, axis=-1, keepdims=True) + 1e-06) * gain


def bucket_of(relative):
    distance = jnp.abs(relative)
    far_part = jnp.full(distance.shape, 8, jnp.int32)
    for edge in bucket_edges:
        far_part = far_part + (distance >= edge).astype(jnp.int32)
    return jnp.where(distance < 8, distance, far_part) + 16 * (relative > 0).astype(jnp.int32)


def position_buckets(length):
    position = jnp.arange(length, dtype=jnp.int32)
    return bucket_of(position[None, :] - position[:, None])


def diagonal_sums(values):
    rows = values.shape[0]
    padded = jnp.concatenate([jnp.zeros((rows, rows), jnp.float32), values], axis=1)
    flat = jnp.concatenate([padded.reshape(-1), jnp.zeros((rows,), jnp.float32)])
    skewed = flat.reshape(rows, 2 * rows + 1)
    return jnp.sum(skewed, axis=0)


def same_sequence(seq_lengths, length):
    position = jnp.arange(length, dtype=jnp.int32)
    ends = jnp.cumsum(seq_lengths)
    segment = jnp.sum((position[:, None] >= ends[None, :]).astype(jnp.int32), axis=1)
    return segment[:, None] == segment[None, :]


def expert_slots(route_ids, capacity):
    onehot = (route_ids[:, None] == jnp.arange(EXPERTS, dtype=jnp.int32)[None, :]).astype(jnp.int32)
    before = jnp.cumsum(onehot, axis=0) - onehot
    slot_of = jnp.sum(before * onehot, axis=1)
    counts = jnp.sum(onehot, axis=0)
    token_of = (
        jnp.zeros((EXPERTS, capacity), jnp.int32)
        .at[route_ids, slot_of]
        .set(jnp.arange(route_ids.shape[0], dtype=jnp.int32))
    )
    filled = jnp.arange(capacity, dtype=jnp.int32)[None, :] < counts[:, None]
    return (slot_of, token_of, filled)


def dot_nt(left, right):
    return lax.dot_general(
        left, right, (((1,), (1,)), ((), ())), preferred_element_type=jnp.float32
    )


def dot_tn(left, right):
    return lax.dot_general(
        left, right, (((0,), (0,)), ((), ())), preferred_element_type=jnp.float32
    )


def gelu_tanh(values):
    return jax.nn.gelu(values, approximate=True)


def on_device(
    tokens,
    gain_attn,
    gain_ffn,
    w_query,
    w_key,
    w_value,
    w_output,
    bias_table,
    router,
    w_in,
    w_out,
    routes,
    lengths,
    cotangent,
):
    tok_count = tokens.shape[0]
    tensor_at = lax.axis_index("tensor")
    group_rows = tok_count * lax.axis_size("tensor")
    capacity = 3 * group_rows // (2 * EXPERTS)
    head_count = w_query.shape[1] // HEAD_DIM
    head_width = w_query.shape[1]
    unit_width = w_in.shape[2]
    full_query, full_key, full_value, full_output = (
        lax.all_gather(w_query, "dp", axis=0, tiled=True),
        lax.all_gather(w_key, "dp", axis=0, tiled=True),
        lax.all_gather(w_value, "dp", axis=0, tiled=True),
        lax.all_gather(w_output, "dp", axis=0, tiled=True),
    )
    tok_f32 = tokens.astype(jnp.float32)
    normed = rms_scale(tok_f32, gain_attn).astype(jnp.bfloat16)
    gathered = lax.all_gather(normed, "tensor", axis=0, tiled=True)
    query = jnp.dot(gathered, full_query, preferred_element_type=jnp.float32).astype(jnp.bfloat16)
    key_proj = jnp.dot(gathered, full_key, preferred_element_type=jnp.float32).astype(jnp.bfloat16)
    value_proj = jnp.dot(gathered, full_value, preferred_element_type=jnp.float32).astype(
        jnp.bfloat16
    )
    same_seq = same_sequence(lengths[0], group_rows)
    bucket = position_buckets(group_rows)
    table_here = lax.dynamic_slice_in_dim(bias_table, tensor_at * head_count, head_count, 1)

    def head_scores(head_at):
        start_col = head_at * HEAD_DIM
        q_part = query[:, start_col : start_col + HEAD_DIM]
        k_part = key_proj[:, start_col : start_col + HEAD_DIM]
        scores = dot_nt(q_part, k_part) + jnp.take(table_here[:, head_at], bucket)
        return jnp.where(same_seq, scores, -1e30)

    head_outputs = []
    log_totals = []
    for head_at in range(head_count):
        scores = head_scores(head_at)
        top = jnp.max(scores, axis=-1, keepdims=True)
        weights = jnp.exp(scores - top)
        total = jnp.sum(weights, axis=-1, keepdims=True)
        log_totals.append(top[:, 0] + jnp.log(total[:, 0]))
        probs = (weights / total).astype(jnp.bfloat16)
        start_col = head_at * HEAD_DIM
        head_outputs.append(
            jnp.dot(
                probs,
                value_proj[:, start_col : start_col + HEAD_DIM],
                preferred_element_type=jnp.float32,
            )
        )
    attended = jnp.concatenate(head_outputs, axis=1).astype(jnp.bfloat16)
    branch = lax.psum_scatter(
        dot_nt(attended, full_output), "tensor", scatter_dimension=0, tiled=True
    )
    middle = tok_f32 + branch
    normed_ffn = rms_scale(middle, gain_ffn).astype(jnp.bfloat16)
    route_ids = routes[:, 0]
    own_routes = lax.dynamic_slice_in_dim(route_ids, tensor_at * tok_count, tok_count)
    own_onehot = (own_routes[:, None] == jnp.arange(EXPERTS, dtype=jnp.int32)[None, :]).astype(
        jnp.float32
    )
    logits = jnp.dot(normed_ffn.astype(jnp.float32), router, precision=highest)
    router_probs = jax.nn.softmax(logits, axis=-1)
    gate = jnp.sum(router_probs * own_onehot, axis=1)
    ffn_rows = lax.all_gather(normed_ffn, "tensor", axis=0, tiled=True)
    slot_of, token_of, filled = expert_slots(route_ids, capacity)
    inputs = jnp.where(filled[..., None], ffn_rows[token_of], jnp.zeros((), jnp.bfloat16))
    expert_in, expert_outw = (
        lax.all_gather(w_in, "dp", axis=0, tiled=True),
        lax.all_gather(w_out, "dp", axis=0, tiled=True),
    )
    pre = jnp.einsum("ecd,def->ecf", inputs, expert_in, preferred_element_type=jnp.float32)
    active = gelu_tanh(pre).astype(jnp.bfloat16)
    expert_out = jnp.einsum("ecf,def->ecd", active, expert_outw, preferred_element_type=jnp.float32)

    def pick_rows(slot_table):
        return slot_table[route_ids, slot_of]

    returned = lax.psum_scatter(pick_rows(expert_out), "tensor", scatter_dimension=0, tiled=True)
    mixed_out = (middle + gate[:, None] * returned).astype(jnp.bfloat16)
    upstream = cotangent.astype(jnp.float32)
    grad_gate = jnp.sum(upstream * returned, axis=1)
    grad_returned = (upstream * gate[:, None]).astype(jnp.bfloat16)
    grad_rows = lax.all_gather(grad_returned, "tensor", axis=0, tiled=True)
    grad_slots = jnp.where(filled[..., None], grad_rows[token_of], jnp.zeros((), jnp.bfloat16))
    grad_active = jnp.einsum(
        "ecd,def->ecf", grad_slots, expert_outw, preferred_element_type=jnp.float32
    )
    gelu_back = jax.vjp(gelu_tanh, pre)[1]
    grad_pre = gelu_back(grad_active)[0].astype(jnp.bfloat16)
    grad_inputs = jnp.einsum(
        "ecf,def->ecd", grad_pre, expert_in, preferred_element_type=jnp.float32
    )
    grad_normed_ffn = lax.psum_scatter(
        pick_rows(grad_inputs), "tensor", scatter_dimension=0, tiled=True
    )
    grad_logits = (grad_gate * gate)[:, None] * (own_onehot - router_probs)
    grad_normed_ffn = grad_normed_ffn + jnp.dot(grad_logits, router.T, precision=highest)
    grad_router = jnp.dot(normed_ffn.astype(jnp.float32).T, grad_logits, precision=highest)
    norm_ffn_back = jax.vjp(rms_scale, middle, gain_ffn)[1]
    grad_middle_norm, grad_gain_ffn = norm_ffn_back(grad_normed_ffn)
    grad_middle = upstream + grad_middle_norm
    grad_branch = lax.all_gather(grad_middle.astype(jnp.bfloat16), "tensor", axis=0, tiled=True)
    grad_attended = jnp.dot(grad_branch, full_output, preferred_element_type=jnp.float32).astype(
        jnp.bfloat16
    )
    offsets = jnp.arange(2 * group_rows + 1, dtype=jnp.int32) - group_rows
    fold_table = (
        bucket_of(offsets)[:, None] == jnp.arange(BUCKETS, dtype=jnp.int32)[None, :]
    ).astype(jnp.float32)
    grad_q_list = []
    grad_k_list = []
    grad_v_list = []
    table_cols = []
    for head_at in range(head_count):
        start_col = head_at * HEAD_DIM
        q_part = query[:, start_col : start_col + HEAD_DIM]
        k_part = key_proj[:, start_col : start_col + HEAD_DIM]
        v_part = value_proj[:, start_col : start_col + HEAD_DIM]
        g_part = grad_attended[:, start_col : start_col + HEAD_DIM]
        probs_f = jnp.exp(head_scores(head_at) - log_totals[head_at][:, None])
        probs_b = probs_f.astype(jnp.bfloat16)
        grad_probs = dot_nt(g_part, v_part)
        row_dot = jnp.sum(grad_probs * probs_f, axis=1, keepdims=True)
        grad_scores = jnp.where(same_seq, probs_f * (grad_probs - row_dot), 0.0).astype(
            jnp.bfloat16
        )
        grad_v_list.append(dot_tn(probs_b, g_part))
        grad_q_list.append(jnp.dot(grad_scores, k_part, preferred_element_type=jnp.float32))
        grad_k_list.append(dot_tn(grad_scores, q_part))
        per_offset = diagonal_sums(grad_scores.astype(jnp.float32))
        table_cols.append(jnp.dot(per_offset, fold_table, precision=highest))
    grad_q = jnp.concatenate(grad_q_list, axis=1).astype(jnp.bfloat16)
    grad_k = jnp.concatenate(grad_k_list, axis=1).astype(jnp.bfloat16)
    grad_v = jnp.concatenate(grad_v_list, axis=1).astype(jnp.bfloat16)
    total_term = dot_nt(grad_q, full_query)
    total_term = total_term + dot_nt(grad_k, full_key)
    grad_normed = lax.psum_scatter(
        (total_term + dot_nt(grad_v, full_value)).astype(jnp.bfloat16),
        "tensor",
        scatter_dimension=0,
        tiled=True,
    ).astype(jnp.float32)
    norm_attn_back = jax.vjp(rms_scale, tok_f32, gain_attn)[1]
    grad_tok_norm, grad_gain_attn = norm_attn_back(grad_normed)
    grad_tokens = grad_middle + grad_tok_norm
    attn_sums = lax.psum_scatter(
        jnp.concatenate(
            [
                dot_tn(gathered, grad_q),
                dot_tn(gathered, grad_k),
                dot_tn(gathered, grad_v),
                dot_tn(grad_branch, attended),
            ],
            axis=1,
        ),
        "dp",
        scatter_dimension=0,
        tiled=True,
    )
    grad_query = attn_sums[:, 0:head_width]
    grad_key = attn_sums[:, head_width : 2 * head_width]
    grad_value = attn_sums[:, 2 * head_width : 3 * head_width]
    grad_output = attn_sums[:, 3 * head_width : 4 * head_width]
    grad_win = jnp.einsum("ecd,ecf->def", inputs, grad_pre, preferred_element_type=jnp.float32)
    grad_wout = jnp.einsum("ecd,ecf->def", grad_slots, active, preferred_element_type=jnp.float32)
    expert_sums = lax.psum_scatter(
        jnp.concatenate([grad_win, grad_wout], axis=2), "dp", scatter_dimension=0, tiled=True
    )
    grad_in = expert_sums[:, :, 0:unit_width]
    grad_out = expert_sums[:, :, unit_width : 2 * unit_width]
    table_grad = lax.dynamic_update_slice_in_dim(
        jnp.zeros(bias_table.shape, jnp.float32),
        jnp.stack(table_cols, axis=1),
        tensor_at * head_count,
        1,
    )
    sum_gain_attn, sum_gain_ffn, sum_table, sum_router = lax.psum(
        (grad_gain_attn, grad_gain_ffn, table_grad, grad_router), ("dp", "tensor")
    )
    return (
        mixed_out,
        grad_tokens,
        sum_gain_attn,
        sum_gain_ffn,
        grad_query,
        grad_key,
        grad_value,
        grad_output,
        sum_table,
        sum_router,
        grad_in,
        grad_out,
    )

class Links:
    def __init__(self, send_sem, recv_sem):
        self.send_sem, self.recv_sem, self.used = send_sem, recv_sem, 0

    def take(self, count):
        first = self.used
        self.used += count
        return first

    def copy(self, index, src, dst, device):
        return pltpu.make_async_remote_copy(
            src_ref=src,
            dst_ref=dst,
            send_sem=self.send_sem.at[index],
            recv_sem=self.recv_sem.at[index],
            device_id=device,
            device_id_type=pl.DeviceIdType.MESH,
        )


def line_gather(links, buf, at, count):
    right, left = links.take(count - 1), links.take(count - 1)

    def to_right(k, shard):
        return links.copy(right + k, buf.at[shard], buf.at[shard], {"tensor": at + 1})

    def to_left(k, shard):
        return links.copy(left + k, buf.at[shard], buf.at[shard], {"tensor": at - 1})

    def step(k):
        @pl.when((at - k >= 0) & (at + 1 < count))
        def _():
            if k > 0:
                to_right(k - 1, at - k).wait_recv()
            to_right(k, at - k).start()

        @pl.when((at + k < count) & (at >= 1))
        def _():
            if k > 0:
                to_left(k - 1, at + k).wait_recv()
            to_left(k, at + k).start()

    def finish():
        for k in range(1, count):

            @pl.when(at == count - 1)
            def _():
                to_right(k - 1, at - k).wait_recv()

            @pl.when(at == 0)
            def _():
                to_left(k - 1, at + k).wait_recv()

        for k in range(count - 1):

            @pl.when((at - k >= 0) & (at + 1 < count))
            def _():
                to_right(k, at - k).wait_send()

            @pl.when((at + k < count) & (at >= 1))
            def _():
                to_left(k, at + k).wait_send()

    return step, finish


def line_scatter(links, part, send_r, send_l, recv_r, recv_l, at, count):
    right, left = links.take(count - 1), links.take(count - 1)

    def to_right(slot):
        return links.copy(right + slot, send_r.at[slot], recv_r.at[slot], {"tensor": at + 1})

    def to_left(slot):
        return links.copy(left + slot, send_l.at[slot], recv_l.at[slot], {"tensor": at - 1})

    def add(one, other):
        return (one.astype(jnp.float32) + other.astype(jnp.float32)).astype(jnp.bfloat16)

    def step(k):
        d = count - 1 - k

        @pl.when(at + d < count)
        def _():
            if d < count - 1:

                @pl.when(at > 0)
                def _():
                    to_right(d).wait_recv()
                    send_r[d - 1] = add(part[at + d], recv_r[d])

                @pl.when(at == 0)
                def _():
                    send_r[d - 1] = part[at + d]
            else:
                send_r[d - 1] = part[at + d]
            to_right(d - 1).start()

        @pl.when(at - d >= 0)
        def _():
            if d < count - 1:

                @pl.when(at < count - 1)
                def _():
                    to_left(d).wait_recv()
                    send_l[d - 1] = add(part[at - d], recv_l[d])

                @pl.when(at == count - 1)
                def _():
                    send_l[d - 1] = part[at - d]
            else:
                send_l[d - 1] = part[at - d]
            to_left(d - 1).start()

    def finish(total):
        total[...] = part[at].astype(jnp.float32)

        @pl.when(at > 0)
        def _():
            to_right(0).wait_recv()
            total[...] += recv_r[0].astype(jnp.float32)

        @pl.when(at < count - 1)
        def _():
            to_left(0).wait_recv()
            total[...] += recv_l[0].astype(jnp.float32)

        for d in range(1, count):

            @pl.when(at + d < count)
            def _():
                to_right(d - 1).wait_send()

            @pl.when(at - d >= 0)
            def _():
                to_left(d - 1).wait_send()

    return step, finish


class ChipGather:
    def __init__(self, links, own, buf, me, chips):
        self.links, self.own, self.buf, self.me, self.chips = links, own, buf, me, chips
        self.chip, self.core = me // 2, me % 2
        self.mate = self.chip * 2 + 1 - self.core
        self.first = links.take(2 * chips)

    def peer(self, k):
        return ((self.chip + k) % self.chips) * 2 + self.core

    def source(self, k):
        return ((self.chip - k + self.chips) % self.chips) * 2 + self.core

    def send(self, k):
        target = self.mate if k == 0 else self.peer(k)
        return self.links.copy(
            self.first + k, self.own, self.buf.at[self.me], {"dp": target}
        )

    def hand_over(self, k):
        shard = self.buf.at[self.source(k)]
        return self.links.copy(self.first + self.chips + k, shard, shard, {"dp": self.mate})

    def start(self):
        for k in range(self.chips):
            self.send(k).start()

    def forward(self):
        for k in range(1, self.chips):
            self.send(k).wait_recv()
            self.hand_over(k).start()

    def finish(self):
        self.send(0).wait_recv()
        for k in range(1, self.chips):
            self.hand_over(k).wait_recv()
        for k in range(self.chips):
            self.send(k).wait_send()
        for k in range(1, self.chips):
            self.hand_over(k).wait_send()


class ChipScatter:
    def __init__(self, links, part, from_mate, from_chips, me, chips):
        self.links, self.part, self.from_mate = links, part, from_mate
        self.summed, self.from_chips, self.chips = from_mate, from_chips, chips
        self.chip, self.core = me // 2, me % 2
        self.mate = self.chip * 2 + 1 - self.core
        self.first = links.take(2 * chips)

    def chip_at(self, k):
        return (self.chip + k) % self.chips

    def swap(self, k):
        return self.links.copy(
            self.first + k,
            self.part.at[self.chip_at(k) * 2 + 1 - self.core],
            self.from_mate.at[k],
            {"dp": self.mate},
        )

    def cross(self, k):
        return self.links.copy(
            self.first + self.chips + k,
            self.summed.at[k],
            self.from_chips.at[k - 1],
            {"dp": self.chip_at(k) * 2 + self.core},
        )

    def start(self):
        for k in range(1, self.chips):
            self.swap(k).start()
        self.swap(0).start()

    def middle(self):
        for k in list(range(1, self.chips)) + [0]:
            self.swap(k).wait_recv()
            mine = self.part.at[self.chip_at(k) * 2 + self.core]

            @pl.loop(0, self.part.shape[1])
            def _(row):
                self.summed[k, row] = (
                    mine[row].astype(jnp.float32) + self.from_mate[k, row].astype(jnp.float32)
                ).astype(jnp.bfloat16)

            if k > 0:
                self.cross(k).start()

    def finish(self, out):
        for k in range(1, self.chips):
            self.cross(k).wait_recv()

        @pl.loop(0, self.part.shape[1])
        def _(row):
            total = self.summed[0, row].astype(jnp.float32)
            for k in range(1, self.chips):
                total = total + self.from_chips[k - 1, row].astype(jnp.float32)
            out[row] = total

        for k in range(self.chips):
            self.swap(k).wait_send()
        for k in range(1, self.chips):
            self.cross(k).wait_send()


def gelu_both(v):
    c = 0.7978845608028654
    sq = v * v
    th = jnp.tanh(c * v * (1.0 + 0.044715 * sq))
    half = 0.5 * (1.0 + th)
    slope = half + 0.5 * v * (1.0 - th * th) * c * (1.0 + 3 * 0.044715 * sq)
    return v * half, slope


def rms_back(values, gain, grad):
    scale = lax.rsqrt(jnp.mean(values * values, axis=-1, keepdims=True) + 1e-06)
    lifted = grad * gain
    inner = jnp.mean(lifted * values, axis=-1, keepdims=True)
    return scale * lifted - values * (scale * scale * scale * inner), jnp.sum(
        grad * values * scale, axis=0, keepdims=True
    )


def layer_kernel(
    chips,
    n_t,
    heads,
    tok,
    cot,
    gains,
    attn_own,
    exp_own,
    table,
    router,
    routes,
    lengths,
    mixed_out,
    gtok_out,
    small_out,
    attn_out,
    exp_out,
    xg,
    cg,
    fg,
    bg,
    aw,
    ew,
    q3,
    k3,
    v3,
    att,
    probs,
    bias,
    seg_col,
    pick,
    slots,
    gslots,
    active,
    slope,
    gpre,
    eo,
    gcols,
    part_b,
    part_r,
    part_g,
    part_n,
    pass_buf,
    total,
    middle,
    gmid,
    gq3,
    gk3,
    gv3,
    gk_acc,
    gv_acc,
    diag,
    gexp,
    gexp_mate,
    gexp_chips,
    gatt,
    gatt_mate,
    gatt_chips,
    small,
    small_t,
    small_m,
    small_in,
    send_sem,
    recv_sem,
):
    bf, f32 = jnp.bfloat16, jnp.float32
    me, at = lax.axis_index("dp"), lax.axis_index("tensor")
    links = Links(send_sem, recv_sem)
    rows, width = tok.shape
    size = n_t * rows
    cap = slots.shape[1]
    chip, core = me // 2, me % 2
    mate = chip * 2 + 1 - core

    def chip_peer(k):
        return ((chip + k) % chips) * 2 + core

    barrier = pltpu.get_barrier_semaphore()
    for k in range(1, n_t):
        pl.semaphore_signal(
            barrier, 1, device_id={"tensor": (at + k) % n_t}, device_id_type=pl.DeviceIdType.MESH
        )
    for k in range(chips):
        pl.semaphore_signal(
            barrier,
            1,
            device_id={"dp": mate if k == 0 else chip_peer(k)},
            device_id_type=pl.DeviceIdType.MESH,
        )
    gain_a, gain_f = gains[0:1, :], gains[1:2, :]
    x_own = tok[...].astype(f32)
    xg[at] = rms_scale(x_own, gain_a).astype(bf)
    cg[at] = cot[...]
    pl.semaphore_wait(barrier, n_t - 1 + chips)

    x_step, x_end = line_gather(links, xg, at, n_t)
    c_step, c_end = line_gather(links, cg, at, n_t)
    f_step, f_end = line_gather(links, fg, at, n_t)
    b_step, b_end = line_gather(links, bg, at, n_t)
    attn_w = ChipGather(links, attn_own, aw, me, chips)
    exp_w = ChipGather(links, exp_own, ew, me, chips)
    x_step(0)
    attn_w.start()
    exp_w.start()
    aw[me] = attn_own[...]
    for i in range(4):
        ew[me, i] = exp_own[i]

    lane = lax.broadcasted_iota(jnp.int32, (BUCKETS, 2 * size), 1)
    offset = jnp.where(lane < size, lane, lane - 2 * size)
    hit = (bucket_of(offset) == lax.broadcasted_iota(jnp.int32, (BUCKETS, 2 * size), 0)).astype(f32)
    for h in range(heads):
        by_offset = jnp.sum(hit * table[:, h : h + 1], axis=0, keepdims=True)
        for s in range(n_t):
            wide = jnp.broadcast_to(by_offset, (rows, 2 * size))
            bias[h, pl.ds(s * rows, rows)] = pltpu.roll(
                wide, s * rows, 1, stride=1, stride_axis=0
            )[:, :size]
    ends = [lengths[0, 0]]
    for s in range(1, lengths.shape[1]):
        ends.append(ends[-1] + lengths[0, s])

    def segments(position):
        seg = jnp.zeros(position.shape, jnp.int32)
        for end in ends:
            seg = seg + (position >= end).astype(jnp.int32)
        return seg

    seg_row = segments(lax.broadcasted_iota(jnp.int32, (1, size), 1))
    seg_col[...] = segments(lax.broadcasted_iota(jnp.int32, (size, 1), 0))
    x_step(1)
    route = routes[...]
    onehot = route == lax.broadcasted_iota(jnp.int32, (size, 128), 1)
    lower = (
        lax.broadcasted_iota(jnp.int32, (size, size), 1)
        < lax.broadcasted_iota(jnp.int32, (size, size), 0)
    ).astype(f32).astype(bf)
    before = jnp.dot(lower, onehot.astype(f32).astype(bf), preferred_element_type=f32)
    place = jnp.sum(jnp.where(onehot, before, 0.0), axis=1, keepdims=True).astype(jnp.int32)
    place = place + route * cap
    pick[...] = (
        (place == lax.broadcasted_iota(jnp.int32, (size, EXPERTS * cap), 1)).astype(f32).astype(bf)
    )
    for k in range(2, n_t - 1):
        x_step(k)
    attn_w.forward()
    x_end()
    c_step(0)
    attn_w.finish()

    def attn_weight(i):
        return aw[:, i].reshape(width, heads * HEAD_DIM)

    @pl.loop(0, n_t)
    def _(s):
        for i, dest in enumerate((q3, k3, v3)):
            made = jnp.dot(xg[s], attn_weight(i), preferred_element_type=f32).astype(bf)
            for h in range(heads):
                dest[h, pl.ds(pl.multiple_of(s * rows, rows), rows)] = made[
                    :, h * HEAD_DIM : (h + 1) * HEAD_DIM
                ]

    c_step(1)

    @pl.loop(0, n_t)
    def _(s):
        here = pl.ds(pl.multiple_of(s * rows, rows), rows)
        same = seg_col[here] == seg_row
        for h in range(heads):
            scores = dot_nt(q3[h, here], k3[h]) + bias[h, here]
            scores = jnp.where(same, scores, -1e30)
            weights = jnp.exp(scores - jnp.max(scores, axis=-1, keepdims=True))
            p = weights * (1.0 / jnp.sum(weights, axis=-1, keepdims=True))
            probs[h, here] = p
            att[here, h * HEAD_DIM : (h + 1) * HEAD_DIM] = jnp.dot(
                p.astype(bf), v3[h], preferred_element_type=f32
            ).astype(bf)
        part_b[s] = dot_nt(att[here], attn_weight(3)).astype(bf)

    def scatter(i, part):
        return line_scatter(
            links, part, pass_buf.at[i, 0], pass_buf.at[i, 1], pass_buf.at[i, 2],
            pass_buf.at[i, 3], at, n_t,
        )

    br_step, br_end = scatter(0, part_b)
    gn_step, gn_end = scatter(1, part_g)
    re_step, re_end = scatter(2, part_r)
    at_step, at_end = scatter(3, part_n)
    for k in range(n_t - 1):
        br_step(k)
    for k in range(2, n_t - 1):
        c_step(k)
    br_end(total)
    middle[...] = tok[...].astype(f32) + total[...]
    fg[at] = rms_scale(middle[...], gain_f).astype(bf)
    f_step(0)
    c_end()
    exp_w.forward()
    for k in range(1, n_t - 1):
        f_step(k)
    f_end()

    def block(s):
        return pl.ds(pl.multiple_of(s * rows, rows), rows)

    @pl.loop(0, n_t)
    def _(s):
        values = fg[s].astype(f32)
        first = jnp.sum(values * router[0:1, :], axis=1, keepdims=True)
        second = jnp.sum(values * router[1:2, :], axis=1, keepdims=True)
        most = jnp.maximum(first, second)
        first, second = jnp.exp(first - most), jnp.exp(second - most)
        whole = 1.0 / (first + second)
        first, second = first * whole, second * whole
        is_second = (routes[block(s)] == 1).astype(f32)
        gate = jnp.where(is_second > 0.5, second, first)
        gcols[0, block(s)] = gate
        gcols[1, block(s)] = 1.0 - is_second - first
        gcols[2, block(s)] = is_second - second
        bg[s] = (cg[s].astype(f32) * gate).astype(bf)

    ffn_rows = fg[...].reshape(size, width)
    grad_rows = bg[...].reshape(size, width)
    for e in range(EXPERTS):
        chosen = pick[:, e * cap : (e + 1) * cap]
        slots[e] = dot_tn(chosen, ffn_rows).astype(bf)
        gslots[e] = dot_tn(chosen, grad_rows).astype(bf)
    exp_w.finish()
    cols = 256
    units = ew.shape[3]
    shard_rows = ew.shape[2]
    half = ew.shape[0] // 2
    wide_half = half * shard_rows

    def tile(j):
        return pl.ds(pl.multiple_of(j * cols, cols), cols)

    for e in range(EXPERTS):

        @pl.loop(0, units // cols)
        def _(j):
            pre = jnp.dot(
                slots[e], ew[:, e, :, tile(j)].reshape(width, cols), preferred_element_type=f32
            )
            value, rate = gelu_both(pre)
            active[e, :, tile(j)] = value.astype(bf)
            slope[e, :, tile(j)] = rate

    for e in range(EXPERTS):
        for j in range(2):
            eo[e, :, j * wide_half : (j + 1) * wide_half] = dot_nt(
                active[e], ew[j * half : (j + 1) * half, 2 + e].reshape(wide_half, units)
            ).astype(bf)

    @pl.loop(0, n_t)
    def _(s):
        back = jnp.dot(
            pick[block(s)], eo[...].reshape(EXPERTS * cap, width), preferred_element_type=f32
        )
        part_r[s] = back.astype(bf)
        gcols[3, block(s)] = (
            jnp.sum(cg[s].astype(f32) * back, axis=1, keepdims=True) * gcols[0, block(s)]
        )

    for e in range(EXPERTS):

        @pl.loop(0, units // cols)
        def _(j):
            grad_active = jnp.dot(
                gslots[e], ew[:, 2 + e, :, tile(j)].reshape(width, cols), preferred_element_type=f32
            )
            gpre[e, :, tile(j)] = (grad_active * slope[e, :, tile(j)]).astype(bf)

    for e in range(EXPERTS):
        for j in range(2):
            eo[e, :, j * wide_half : (j + 1) * wide_half] = dot_nt(
                gpre[e], ew[j * half : (j + 1) * half, e].reshape(wide_half, units)
            ).astype(bf)
    small[...] = jnp.zeros_like(small)

    @pl.loop(0, n_t)
    def _(s):
        back = jnp.dot(
            pick[block(s)], eo[...].reshape(EXPERTS * cap, width), preferred_element_type=f32
        )
        values = fg[s].astype(f32)
        for e in range(EXPERTS):
            grad_logit = gcols[3, block(s)] * gcols[1 + e, block(s)]
            back = back + grad_logit * router[e : e + 1, :]
            small[2 + e : 3 + e, :] += jnp.sum(values * grad_logit, axis=0, keepdims=True)
        part_g[s] = back.astype(bf)

    exp_g = ChipScatter(links, gexp, gexp_mate, gexp_chips, me, chips)
    gn_step(0)

    def weight_grads(left, right, i):
        @pl.loop(0, units // cols)
        def _(j):
            gexp[:, i, :, tile(j)] = (
                dot_tn(left, right[:, tile(j)]).astype(bf).reshape(2 * half, shard_rows, cols)
            )

    for e in range(EXPERTS):
        weight_grads(slots[e], gpre.at[e], e)
    for k in range(1, n_t - 2):
        gn_step(k)
    for e in range(EXPERTS):
        weight_grads(gslots[e], active.at[e], 2 + e)
    for k in range(max(1, n_t - 2), n_t - 1):
        gn_step(k)
    exp_g.start()
    gn_end(total)
    norm_back, gain_part = rms_back(middle[...], gain_f, total[...])
    small[1:2, :] = gain_part
    grad_mid = cot[...].astype(f32) + norm_back
    gmid[...] = grad_mid
    bg[at] = grad_mid.astype(bf)
    b_step(0)
    exp_g.middle()
    for k in range(1, n_t - 1):
        b_step(k)
    b_end()
    re_step(0)

    diag[...] = jnp.zeros_like(diag)
    gk_acc[...] = jnp.zeros_like(gk_acc)
    gv_acc[...] = jnp.zeros_like(gv_acc)
    mirror = (
        lax.broadcasted_iota(jnp.int32, (rows, rows), 0)
        + lax.broadcasted_iota(jnp.int32, (rows, rows), 1)
        == rows - 1
    ).astype(f32).astype(bf)

    def attn_back(s):
        here = block(s)
        same = seg_col[here] == seg_row
        grad_att = jnp.dot(bg[s], attn_weight(3), preferred_element_type=f32).astype(bf)
        for h in range(heads):
            g_part = grad_att[:, h * HEAD_DIM : (h + 1) * HEAD_DIM]
            p = probs[h, here]
            grad_p = dot_nt(g_part, v3[h])
            row_dot = jnp.sum(grad_p * p, axis=1, keepdims=True)
            grad_s = jnp.where(same, p * (grad_p - row_dot), 0.0).astype(bf)
            gv_acc[h] += dot_tn(p.astype(bf), g_part)
            gk_acc[h] += dot_tn(grad_s, q3[h, here])
            gq3[here, h * HEAD_DIM : (h + 1) * HEAD_DIM] = jnp.dot(
                grad_s, k3[h], preferred_element_type=f32
            ).astype(bf)
            turned = jnp.dot(mirror, grad_s, preferred_element_type=f32)
            turned = jnp.concatenate([turned, jnp.zeros((rows, rows), f32)], axis=1)
            turned = pltpu.roll(turned, 0, 1, stride=1, stride_axis=0)
            folded = jnp.sum(turned.reshape(rows // 8, 8, size + rows), axis=0)
            base = pl.multiple_of(size - rows - s * rows, rows)
            diag[h, :, pl.ds(base, size + rows)] += folded

    @pl.loop(0, n_t // 2)
    def _(s):
        attn_back(s)

    for k in range(1, n_t - 2):
        re_step(k)

    @pl.loop(n_t // 2, n_t)
    def _(s):
        attn_back(s)

    for h in range(heads):
        gk3[:, h * HEAD_DIM : (h + 1) * HEAD_DIM] = gk_acc[h].astype(bf)
        gv3[:, h * HEAD_DIM : (h + 1) * HEAD_DIM] = gv_acc[h].astype(bf)

    @pl.loop(0, n_t)
    def _(s):
        back = dot_nt(gq3[block(s)], attn_weight(0))
        back = back + dot_nt(gk3[block(s)], attn_weight(1))
        back = back + dot_nt(gv3[block(s)], attn_weight(2))
        part_n[s] = back.astype(bf)
        small[0:1, :] += jnp.sum(back * xg[s].astype(f32), axis=0, keepdims=True)

    at_step(0)
    small[0:1, :] = small[0:1, :] / gain_a
    spot = lax.broadcasted_iota(jnp.int32, (2 * size, 128), 0) - (size - 1)
    fold = (bucket_of(spot) == lax.broadcasted_iota(jnp.int32, (2 * size, 128), 1)).astype(f32)
    line = lax.broadcasted_iota(jnp.int32, (small.shape[0], 128), 0)
    for h in range(heads):
        sums = jnp.dot(diag[h], fold, precision=highest, preferred_element_type=f32)
        sums = jnp.sum(sums, axis=0, keepdims=True)
        small[:, 0:128] += jnp.where(line == 4 + at * heads + h, sums, 0.0)

    first = links.take(n_t - 1)

    def small_line(k):
        return links.copy(first + k - 1, small, small_t.at[k - 1], {"tensor": (at + k) % n_t})

    for k in range(1, n_t):
        small_line(k).start()
    att_g = ChipScatter(links, gatt, gatt_mate, gatt_chips, me, chips)
    normed = xg[...].reshape(size, width)
    shape = (2 * half, shard_rows, heads * HEAD_DIM)
    gatt[:, 0] = dot_tn(normed, gq3[...]).astype(bf).reshape(shape)
    gatt[:, 1] = dot_tn(normed, gk3[...]).astype(bf).reshape(shape)
    for k in range(1, n_t - 2):
        at_step(k)
    gatt[:, 2] = dot_tn(normed, gv3[...]).astype(bf).reshape(shape)
    gatt[:, 3] = dot_tn(bg[...].reshape(size, width), att[...]).astype(bf).reshape(shape)
    att_g.start()
    for k in range(max(1, n_t - 2), n_t - 1):
        at_step(k)
    joined = small[...]
    for k in range(1, n_t):
        small_line(k).wait_recv()
        joined = joined + small_t[k - 1]
    small_m[0] = joined
    second = links.take(chips)
    swap = links.copy(second, small_m.at[0], small_in.at[0], {"dp": mate})
    swap.start()
    att_g.middle()
    swap.wait_recv()
    small_m[1] = small_m[0] + small_in[0]

    def small_chip(k):
        return links.copy(second + k, small_m.at[1], small_in.at[k], {"dp": chip_peer(k)})

    for k in range(1, chips):
        small_chip(k).start()
    for k in range(max(1, n_t - 2), n_t - 1):
        re_step(k)
    exp_g.finish(exp_out)
    at_end(total)
    tok_back, _ = rms_back(tok[...].astype(f32), gain_a, total[...])
    gtok_out[...] = gmid[...] + tok_back
    re_end(total)
    own_gate = gcols[0, block(at)]
    mixed_out[...] = (middle[...] + own_gate * total[...]).astype(bf)
    joined = small_m[1]
    for k in range(1, chips):
        small_chip(k).wait_recv()
        joined = joined + small_in[k]
    small_out[...] = joined
    att_g.finish(attn_out)
    for k in range(1, n_t):
        small_line(k).wait_send()
    swap.wait_send()
    for k in range(1, chips):
        small_chip(k).wait_send()


def fused_layer(
    tokens, gain_attn, gain_ffn, w_query, w_key, w_value, w_output, bias_table, router,
    w_in, w_out, routes, lengths, cotangent,
):
    bf, f32 = jnp.bfloat16, jnp.float32
    n_dp, n_t = lax.axis_size("dp"), lax.axis_size("tensor")
    chips = n_dp // 2
    rows, width = tokens.shape
    size = rows * n_t
    cap = 3 * size // (2 * EXPERTS)
    shard, head_width = w_query.shape
    heads = head_width // HEAD_DIM
    units = w_in.shape[2]
    all_heads = bias_table.shape[1]
    small_rows = -(-(4 + all_heads) // 8) * 8
    attn_own = jnp.stack([w_query, w_key, w_value, w_output])
    exp_own = jnp.concatenate([w_in.transpose(1, 0, 2), w_out.transpose(1, 0, 2)], axis=0)
    table = lax.dynamic_slice_in_dim(bias_table, lax.axis_index("tensor") * heads, heads, 1)
    vm = pl.BlockSpec(memory_space=pltpu.VMEM)
    V = pltpu.VMEM
    group = (n_t, rows, width)
    scratch = [
        V(group, bf), V(group, bf), V(group, bf), V(group, bf),
        V((n_dp, 4, shard, head_width), bf), V((n_dp, 4, shard, units), bf),
        V((heads, size, HEAD_DIM), bf), V((heads, size, HEAD_DIM), bf),
        V((heads, size, HEAD_DIM), bf),
        V((size, head_width), bf),
        V((heads, size, size), f32), V((heads, size, size), f32),
        V((size, 1), jnp.int32), V((size, EXPERTS * cap), bf),
        V((EXPERTS, cap, width), bf), V((EXPERTS, cap, width), bf),
        V((EXPERTS, cap, units), bf), V((EXPERTS, cap, units), f32), V((EXPERTS, cap, units), bf),
        V((EXPERTS, cap, width), bf), V((4, size, 1), f32),
        V(group, bf), V(group, bf), V(group, bf), V(group, bf),
        V((4, 4, n_t - 1, rows, width), bf),
        V((rows, width), f32), V((rows, width), f32), V((rows, width), f32),
        V((size, head_width), bf), V((size, head_width), bf), V((size, head_width), bf),
        V((heads, size, HEAD_DIM), f32), V((heads, size, HEAD_DIM), f32),
        V((heads, 8, 2 * size), f32),
        V((n_dp, 4, shard, units), bf), V((chips, 4, shard, units), bf),
        V((chips - 1, 4, shard, units), bf),
        V((n_dp, 4, shard, head_width), bf), V((chips, 4, shard, head_width), bf),
        V((chips - 1, 4, shard, head_width), bf),
        V((small_rows, width), f32), V((n_t - 1, small_rows, width), f32),
        V((2, small_rows, width), f32), V((chips, small_rows, width), f32),
        pltpu.SemaphoreType.DMA((96,)), pltpu.SemaphoreType.DMA((96,)),
    ]
    mixed, grad_tok, small, attn_g, exp_g = pl.pallas_call(
        functools.partial(layer_kernel, chips, n_t, heads),
        out_shape=(
            jax.ShapeDtypeStruct((rows, width), bf),
            jax.ShapeDtypeStruct((rows, width), f32),
            jax.ShapeDtypeStruct((small_rows, width), f32),
            jax.ShapeDtypeStruct((4, shard, head_width), f32),
            jax.ShapeDtypeStruct((4, shard, units), f32),
        ),
        in_specs=[vm] * 8 + [pl.BlockSpec(memory_space=pltpu.SMEM)],
        out_specs=[vm] * 5,
        scratch_shapes=scratch,
        compiler_params=pltpu.CompilerParams(
            collective_id=0, has_side_effects=True, vmem_limit_bytes=60 * 1024 * 1024
        ),
    )(
        tokens, cotangent, jnp.stack([gain_attn, gain_ffn]), attn_own, exp_own, table,
        router.T, routes, lengths,
    )
    return (
        mixed, grad_tok, small[0], small[1], attn_g[0], attn_g[1], attn_g[2], attn_g[3],
        small[4 : 4 + all_heads, :BUCKETS].T, small[2:4].T,
        exp_g[0:2].transpose(1, 0, 2), exp_g[2:4].transpose(1, 0, 2),
    )


def solution(mesh):
    in_specs = (
        P(("dp", "tensor"), None),
        P(),
        P(),
        P("dp", "tensor"),
        P("dp", "tensor"),
        P("dp", "tensor"),
        P("dp", "tensor"),
        P(),
        P(),
        P("dp", None, "tensor"),
        P("dp", None, "tensor"),
        P("dp", None),
        P("dp", None),
        P(("dp", "tensor"), None),
    )
    out_specs = (
        P(("dp", "tensor"), None),
        P(("dp", "tensor"), None),
        P(),
        P(),
        P("dp", "tensor"),
        P("dp", "tensor"),
        P("dp", "tensor"),
        P("dp", "tensor"),
        P(),
        P(),
        P("dp", None, "tensor"),
        P("dp", None, "tensor"),
    )

    def layer(*arrays):
        shard_rows, chips = arrays[3].shape[0], mesh.shape["dp"] // 2
        fits = shard_rows % 16 == 0 and mesh.shape["dp"] == 2 * chips and chips > 1
        return (fused_layer if fits else on_device)(*arrays)

    return jax.shard_map(
        layer, mesh=mesh, in_specs=in_specs, out_specs=out_specs, check_vma=False
    )
```

```python
import functools

import jax
import jax.numpy as jnp
from jax import lax
from jax.experimental import pallas as pl
from jax.experimental.pallas import tpu as pltpu
from jax.sharding import PartitionSpec as P

HEAD_DIM = 64
EXPERTS = 2
BUCKETS = 32
PIECES = 2


highest = lax.Precision.HIGHEST
bucket_edges = (12, 16, 23, 32, 46, 64, 91)


def rms_scale(values, gain):
    return values * lax.rsqrt(jnp.mean(values * values, axis=-1, keepdims=True) + 1e-06) * gain


def bucket_of(relative):
    distance = jnp.abs(relative)
    far_part = jnp.full(distance.shape, 8, jnp.int32)
    for edge in bucket_edges:
        far_part = far_part + (distance >= edge).astype(jnp.int32)
    return jnp.where(distance < 8, distance, far_part) + 16 * (relative > 0).astype(jnp.int32)


def position_buckets(length):
    position = jnp.arange(length, dtype=jnp.int32)
    return bucket_of(position[None, :] - position[:, None])


def diagonal_sums(values):
    rows = values.shape[0]
    padded = jnp.concatenate([jnp.zeros((rows, rows), jnp.float32), values], axis=1)
    flat = jnp.concatenate([padded.reshape(-1), jnp.zeros((rows,), jnp.float32)])
    skewed = flat.reshape(rows, 2 * rows + 1)
    return jnp.sum(skewed, axis=0)


def same_sequence(seq_lengths, length):
    position = jnp.arange(length, dtype=jnp.int32)
    ends = jnp.cumsum(seq_lengths)
    segment = jnp.sum((position[:, None] >= ends[None, :]).astype(jnp.int32), axis=1)
    return segment[:, None] == segment[None, :]


def expert_slots(route_ids, capacity):
    onehot = (route_ids[:, None] == jnp.arange(EXPERTS, dtype=jnp.int32)[None, :]).astype(jnp.int32)
    before = jnp.cumsum(onehot, axis=0) - onehot
    slot_of = jnp.sum(before * onehot, axis=1)
    counts = jnp.sum(onehot, axis=0)
    token_of = (
        jnp.zeros((EXPERTS, capacity), jnp.int32)
        .at[route_ids, slot_of]
        .set(jnp.arange(route_ids.shape[0], dtype=jnp.int32))
    )
    filled = jnp.arange(capacity, dtype=jnp.int32)[None, :] < counts[:, None]
    return (slot_of, token_of, filled)


def dot_nt(left, right):
    return lax.dot_general(
        left, right, (((1,), (1,)), ((), ())), preferred_element_type=jnp.float32
    )


def dot_tn(left, right):
    return lax.dot_general(
        left, right, (((0,), (0,)), ((), ())), preferred_element_type=jnp.float32
    )


def gelu_tanh(values):
    return jax.nn.gelu(values, approximate=True)


def on_device(
    tokens,
    gain_attn,
    gain_ffn,
    w_query,
    w_key,
    w_value,
    w_output,
    bias_table,
    router,
    w_in,
    w_out,
    routes,
    lengths,
    cotangent,
):
    tok_count = tokens.shape[0]
    tensor_at = lax.axis_index("tensor")
    group_rows = tok_count * lax.axis_size("tensor")
    capacity = 3 * group_rows // (2 * EXPERTS)
    head_count = w_query.shape[1] // HEAD_DIM
    head_width = w_query.shape[1]
    unit_width = w_in.shape[2]
    full_query, full_key, full_value, full_output = (
        lax.all_gather(w_query, "dp", axis=0, tiled=True),
        lax.all_gather(w_key, "dp", axis=0, tiled=True),
        lax.all_gather(w_value, "dp", axis=0, tiled=True),
        lax.all_gather(w_output, "dp", axis=0, tiled=True),
    )
    tok_f32 = tokens.astype(jnp.float32)
    normed = rms_scale(tok_f32, gain_attn).astype(jnp.bfloat16)
    gathered = lax.all_gather(normed, "tensor", axis=0, tiled=True)
    query = jnp.dot(gathered, full_query, preferred_element_type=jnp.float32).astype(jnp.bfloat16)
    key_proj = jnp.dot(gathered, full_key, preferred_element_type=jnp.float32).astype(jnp.bfloat16)
    value_proj = jnp.dot(gathered, full_value, preferred_element_type=jnp.float32).astype(
        jnp.bfloat16
    )
    same_seq = same_sequence(lengths[0], group_rows)
    bucket = position_buckets(group_rows)
    table_here = lax.dynamic_slice_in_dim(bias_table, tensor_at * head_count, head_count, 1)

    def head_scores(head_at):
        start_col = head_at * HEAD_DIM
        q_part = query[:, start_col : start_col + HEAD_DIM]
        k_part = key_proj[:, start_col : start_col + HEAD_DIM]
        scores = dot_nt(q_part, k_part) + jnp.take(table_here[:, head_at], bucket)
        return jnp.where(same_seq, scores, -1e30)

    head_outputs = []
    log_totals = []
    for head_at in range(head_count):
        scores = head_scores(head_at)
        top = jnp.max(scores, axis=-1, keepdims=True)
        weights = jnp.exp(scores - top)
        total = jnp.sum(weights, axis=-1, keepdims=True)
        log_totals.append(top[:, 0] + jnp.log(total[:, 0]))
        probs = (weights / total).astype(jnp.bfloat16)
        start_col = head_at * HEAD_DIM
        head_outputs.append(
            jnp.dot(
                probs,
                value_proj[:, start_col : start_col + HEAD_DIM],
                preferred_element_type=jnp.float32,
            )
        )
    attended = jnp.concatenate(head_outputs, axis=1).astype(jnp.bfloat16)
    branch = lax.psum_scatter(
        dot_nt(attended, full_output), "tensor", scatter_dimension=0, tiled=True
    )
    middle = tok_f32 + branch
    normed_ffn = rms_scale(middle, gain_ffn).astype(jnp.bfloat16)
    route_ids = routes[:, 0]
    own_routes = lax.dynamic_slice_in_dim(route_ids, tensor_at * tok_count, tok_count)
    own_onehot = (own_routes[:, None] == jnp.arange(EXPERTS, dtype=jnp.int32)[None, :]).astype(
        jnp.float32
    )
    logits = jnp.dot(normed_ffn.astype(jnp.float32), router, precision=highest)
    router_probs = jax.nn.softmax(logits, axis=-1)
    gate = jnp.sum(router_probs * own_onehot, axis=1)
    ffn_rows = lax.all_gather(normed_ffn, "tensor", axis=0, tiled=True)
    slot_of, token_of, filled = expert_slots(route_ids, capacity)
    inputs = jnp.where(filled[..., None], ffn_rows[token_of], jnp.zeros((), jnp.bfloat16))
    expert_in, expert_outw = (
        lax.all_gather(w_in, "dp", axis=0, tiled=True),
        lax.all_gather(w_out, "dp", axis=0, tiled=True),
    )
    pre = jnp.einsum("ecd,def->ecf", inputs, expert_in, preferred_element_type=jnp.float32)
    active = gelu_tanh(pre).astype(jnp.bfloat16)
    expert_out = jnp.einsum("ecf,def->ecd", active, expert_outw, preferred_element_type=jnp.float32)

    def pick_rows(slot_table):
        return slot_table[route_ids, slot_of]

    returned = lax.psum_scatter(pick_rows(expert_out), "tensor", scatter_dimension=0, tiled=True)
    mixed_out = (middle + gate[:, None] * returned).astype(jnp.bfloat16)
    upstream = cotangent.astype(jnp.float32)
    grad_gate = jnp.sum(upstream * returned, axis=1)
    grad_returned = (upstream * gate[:, None]).astype(jnp.bfloat16)
    grad_rows = lax.all_gather(grad_returned, "tensor", axis=0, tiled=True)
    grad_slots = jnp.where(filled[..., None], grad_rows[token_of], jnp.zeros((), jnp.bfloat16))
    grad_active = jnp.einsum(
        "ecd,def->ecf", grad_slots, expert_outw, preferred_element_type=jnp.float32
    )
    gelu_back = jax.vjp(gelu_tanh, pre)[1]
    grad_pre = gelu_back(grad_active)[0].astype(jnp.bfloat16)
    grad_inputs = jnp.einsum(
        "ecf,def->ecd", grad_pre, expert_in, preferred_element_type=jnp.float32
    )
    grad_normed_ffn = lax.psum_scatter(
        pick_rows(grad_inputs), "tensor", scatter_dimension=0, tiled=True
    )
    grad_logits = (grad_gate * gate)[:, None] * (own_onehot - router_probs)
    grad_normed_ffn = grad_normed_ffn + jnp.dot(grad_logits, router.T, precision=highest)
    grad_router = jnp.dot(normed_ffn.astype(jnp.float32).T, grad_logits, precision=highest)
    norm_ffn_back = jax.vjp(rms_scale, middle, gain_ffn)[1]
    grad_middle_norm, grad_gain_ffn = norm_ffn_back(grad_normed_ffn)
    grad_middle = upstream + grad_middle_norm
    grad_branch = lax.all_gather(grad_middle.astype(jnp.bfloat16), "tensor", axis=0, tiled=True)
    grad_attended = jnp.dot(grad_branch, full_output, preferred_element_type=jnp.float32).astype(
        jnp.bfloat16
    )
    offsets = jnp.arange(2 * group_rows + 1, dtype=jnp.int32) - group_rows
    fold_table = (
        bucket_of(offsets)[:, None] == jnp.arange(BUCKETS, dtype=jnp.int32)[None, :]
    ).astype(jnp.float32)
    grad_q_list = []
    grad_k_list = []
    grad_v_list = []
    table_cols = []
    for head_at in range(head_count):
        start_col = head_at * HEAD_DIM
        q_part = query[:, start_col : start_col + HEAD_DIM]
        k_part = key_proj[:, start_col : start_col + HEAD_DIM]
        v_part = value_proj[:, start_col : start_col + HEAD_DIM]
        g_part = grad_attended[:, start_col : start_col + HEAD_DIM]
        probs_f = jnp.exp(head_scores(head_at) - log_totals[head_at][:, None])
        probs_b = probs_f.astype(jnp.bfloat16)
        grad_probs = dot_nt(g_part, v_part)
        row_dot = jnp.sum(grad_probs * probs_f, axis=1, keepdims=True)
        grad_scores = jnp.where(same_seq, probs_f * (grad_probs - row_dot), 0.0).astype(
            jnp.bfloat16
        )
        grad_v_list.append(dot_tn(probs_b, g_part))
        grad_q_list.append(jnp.dot(grad_scores, k_part, preferred_element_type=jnp.float32))
        grad_k_list.append(dot_tn(grad_scores, q_part))
        per_offset = diagonal_sums(grad_scores.astype(jnp.float32))
        table_cols.append(jnp.dot(per_offset, fold_table, precision=highest))
    grad_q = jnp.concatenate(grad_q_list, axis=1).astype(jnp.bfloat16)
    grad_k = jnp.concatenate(grad_k_list, axis=1).astype(jnp.bfloat16)
    grad_v = jnp.concatenate(grad_v_list, axis=1).astype(jnp.bfloat16)
    total_term = dot_nt(grad_q, full_query)
    total_term = total_term + dot_nt(grad_k, full_key)
    grad_normed = lax.psum_scatter(
        (total_term + dot_nt(grad_v, full_value)).astype(jnp.bfloat16),
        "tensor",
        scatter_dimension=0,
        tiled=True,
    ).astype(jnp.float32)
    norm_attn_back = jax.vjp(rms_scale, tok_f32, gain_attn)[1]
    grad_tok_norm, grad_gain_attn = norm_attn_back(grad_normed)
    grad_tokens = grad_middle + grad_tok_norm
    attn_sums = lax.psum_scatter(
        jnp.concatenate(
            [
                dot_tn(gathered, grad_q),
                dot_tn(gathered, grad_k),
                dot_tn(gathered, grad_v),
                dot_tn(grad_branch, attended),
            ],
            axis=1,
        ),
        "dp",
        scatter_dimension=0,
        tiled=True,
    )
    grad_query = attn_sums[:, 0:head_width]
    grad_key = attn_sums[:, head_width : 2 * head_width]
    grad_value = attn_sums[:, 2 * head_width : 3 * head_width]
    grad_output = attn_sums[:, 3 * head_width : 4 * head_width]
    grad_win = jnp.einsum("ecd,ecf->def", inputs, grad_pre, preferred_element_type=jnp.float32)
    grad_wout = jnp.einsum("ecd,ecf->def", grad_slots, active, preferred_element_type=jnp.float32)
    expert_sums = lax.psum_scatter(
        jnp.concatenate([grad_win, grad_wout], axis=2), "dp", scatter_dimension=0, tiled=True
    )
    grad_in = expert_sums[:, :, 0:unit_width]
    grad_out = expert_sums[:, :, unit_width : 2 * unit_width]
    table_grad = lax.dynamic_update_slice_in_dim(
        jnp.zeros(bias_table.shape, jnp.float32),
        jnp.stack(table_cols, axis=1),
        tensor_at * head_count,
        1,
    )
    sum_gain_attn, sum_gain_ffn, sum_table, sum_router = lax.psum(
        (grad_gain_attn, grad_gain_ffn, table_grad, grad_router), ("dp", "tensor")
    )
    return (
        mixed_out,
        grad_tokens,
        sum_gain_attn,
        sum_gain_ffn,
        grad_query,
        grad_key,
        grad_value,
        grad_output,
        sum_table,
        sum_router,
        grad_in,
        grad_out,
    )

class Links:
    def __init__(self, send_sem, recv_sem):
        self.send_sem, self.recv_sem, self.used = send_sem, recv_sem, 0

    def take(self, count):
        first = self.used
        self.used += count
        return first

    def copy(self, index, src, dst, device):
        return pltpu.make_async_remote_copy(
            src_ref=src,
            dst_ref=dst,
            send_sem=self.send_sem.at[index],
            recv_sem=self.recv_sem.at[index],
            device_id=device,
            device_id_type=pl.DeviceIdType.MESH,
        )


def line_gather_piece(links, buf, at, count, here):
    right, left = links.take(count - 1), links.take(count - 1)

    def to_right(k, shard):
        return links.copy(right + k, buf.at[shard, here], buf.at[shard, here], {"tensor": at + 1})

    def to_left(k, shard):
        return links.copy(left + k, buf.at[shard, here], buf.at[shard, here], {"tensor": at - 1})

    def step(k):
        @pl.when((at - k >= 0) & (at + 1 < count))
        def _():
            if k > 0:
                to_right(k - 1, at - k).wait_recv()
            to_right(k, at - k).start()

        @pl.when((at + k < count) & (at >= 1))
        def _():
            if k > 0:
                to_left(k - 1, at + k).wait_recv()
            to_left(k, at + k).start()

    def finish():
        for k in range(1, count):

            @pl.when(at == count - 1)
            def _():
                to_right(k - 1, at - k).wait_recv()

            @pl.when(at == 0)
            def _():
                to_left(k - 1, at + k).wait_recv()

        for k in range(count - 1):

            @pl.when((at - k >= 0) & (at + 1 < count))
            def _():
                to_right(k, at - k).wait_send()

            @pl.when((at + k < count) & (at >= 1))
            def _():
                to_left(k, at + k).wait_send()

    return step, finish


def line_scatter_piece(links, part, send_r, send_l, recv_r, recv_l, at, count, here):
    right, left = links.take(count - 1), links.take(count - 1)

    def to_right(slot):
        return links.copy(right + slot, send_r.at[slot, here], recv_r.at[slot, here], {"tensor": at + 1})

    def to_left(slot):
        return links.copy(left + slot, send_l.at[slot, here], recv_l.at[slot, here], {"tensor": at - 1})

    def add(one, other):
        return (one.astype(jnp.float32) + other.astype(jnp.float32)).astype(jnp.bfloat16)

    def step(k):
        d = count - 1 - k

        @pl.when(at + d < count)
        def _():
            if d < count - 1:

                @pl.when(at > 0)
                def _():
                    to_right(d).wait_recv()
                    send_r[d - 1, here] = add(part[at + d, here], recv_r[d, here])

                @pl.when(at == 0)
                def _():
                    send_r[d - 1, here] = part[at + d, here]
            else:
                send_r[d - 1, here] = part[at + d, here]
            to_right(d - 1).start()

        @pl.when(at - d >= 0)
        def _():
            if d < count - 1:

                @pl.when(at < count - 1)
                def _():
                    to_left(d).wait_recv()
                    send_l[d - 1, here] = add(part[at - d, here], recv_l[d, here])

                @pl.when(at == count - 1)
                def _():
                    send_l[d - 1, here] = part[at - d, here]
            else:
                send_l[d - 1, here] = part[at - d, here]
            to_left(d - 1).start()

    def finish(total):
        total[here] = part[at, here].astype(jnp.float32)

        @pl.when(at > 0)
        def _():
            to_right(0).wait_recv()
            total[here] += recv_r[0, here].astype(jnp.float32)

        @pl.when(at < count - 1)
        def _():
            to_left(0).wait_recv()
            total[here] += recv_l[0, here].astype(jnp.float32)

        for d in range(1, count):

            @pl.when(at + d < count)
            def _():
                to_right(d - 1).wait_send()

            @pl.when(at - d >= 0)
            def _():
                to_left(d - 1).wait_send()

    return step, finish


def in_pieces(make, rows):
    height = rows // PIECES
    made = [make(pl.ds(p * height, height)) for p in range(PIECES)]

    def step(k):
        for one, _ in made:
            one(k)

    def finish(*args):
        for _, last in made:
            last(*args)

    return step, finish


def line_gather(links, buf, at, count):
    return in_pieces(lambda here: line_gather_piece(links, buf, at, count, here), buf.shape[1])


def line_scatter(links, part, send_r, send_l, recv_r, recv_l, at, count):
    return in_pieces(
        lambda here: line_scatter_piece(
            links, part, send_r, send_l, recv_r, recv_l, at, count, here
        ),
        part.shape[1],
    )


class ChipGather:
    def __init__(self, links, own, buf, me, chips):
        self.links, self.own, self.buf, self.me, self.chips = links, own, buf, me, chips
        self.chip, self.core = me // 2, me % 2
        self.mate = self.chip * 2 + 1 - self.core
        self.first = links.take(2 * chips)

    def peer(self, k):
        return ((self.chip + k) % self.chips) * 2 + self.core

    def source(self, k):
        return ((self.chip - k + self.chips) % self.chips) * 2 + self.core

    def send(self, k):
        target = self.mate if k == 0 else self.peer(k)
        return self.links.copy(
            self.first + k, self.own, self.buf.at[self.me], {"dp": target}
        )

    def hand_over(self, k):
        shard = self.buf.at[self.source(k)]
        return self.links.copy(self.first + self.chips + k, shard, shard, {"dp": self.mate})

    def start(self):
        for k in range(self.chips):
            self.send(k).start()

    def forward(self):
        for k in range(1, self.chips):
            self.send(k).wait_recv()
            self.hand_over(k).start()

    def finish(self):
        self.send(0).wait_recv()
        for k in range(1, self.chips):
            self.hand_over(k).wait_recv()
        for k in range(self.chips):
            self.send(k).wait_send()
        for k in range(1, self.chips):
            self.hand_over(k).wait_send()


class ChipScatter:
    def __init__(self, links, part, from_mate, from_chips, me, chips):
        self.links, self.part, self.from_mate = links, part, from_mate
        self.summed, self.from_chips, self.chips = from_mate, from_chips, chips
        self.chip, self.core = me // 2, me % 2
        self.mate = self.chip * 2 + 1 - self.core
        self.first = links.take(2 * chips)

    def chip_at(self, k):
        return (self.chip + k) % self.chips

    def swap(self, k):
        return self.links.copy(
            self.first + k,
            self.part.at[self.chip_at(k) * 2 + 1 - self.core],
            self.from_mate.at[k],
            {"dp": self.mate},
        )

    def cross(self, k):
        return self.links.copy(
            self.first + self.chips + k,
            self.summed.at[k],
            self.from_chips.at[k - 1],
            {"dp": self.chip_at(k) * 2 + self.core},
        )

    def start(self):
        for k in range(1, self.chips):
            self.swap(k).start()
        self.swap(0).start()

    def middle(self):
        for k in list(range(1, self.chips)) + [0]:
            self.swap(k).wait_recv()
            mine = self.part.at[self.chip_at(k) * 2 + self.core]

            @pl.loop(0, self.part.shape[1])
            def _(row):
                self.summed[k, row] = (
                    mine[row].astype(jnp.float32) + self.from_mate[k, row].astype(jnp.float32)
                ).astype(jnp.bfloat16)

            if k > 0:
                self.cross(k).start()

    def finish(self, outs):
        for k in range(1, self.chips):
            self.cross(k).wait_recv()
        for row, out in enumerate(outs):
            total = self.summed[0, row].astype(jnp.float32)
            for k in range(1, self.chips):
                total = total + self.from_chips[k - 1, row].astype(jnp.float32)
            out[...] = total

        for k in range(self.chips):
            self.swap(k).wait_send()
        for k in range(1, self.chips):
            self.cross(k).wait_send()


def gelu_both(v):
    c = 0.7978845608028654
    sq = v * v
    th = jnp.tanh(c * v * (1.0 + 0.044715 * sq))
    half = 0.5 * (1.0 + th)
    slope = half + 0.5 * v * (1.0 - th * th) * c * (1.0 + 3 * 0.044715 * sq)
    return v * half, slope


def rms_back(values, gain, grad):
    scale = lax.rsqrt(jnp.mean(values * values, axis=-1, keepdims=True) + 1e-06)
    lifted = grad * gain
    inner = jnp.mean(lifted * values, axis=-1, keepdims=True)
    return scale * lifted - values * (scale * scale * scale * inner), jnp.sum(
        grad * values * scale, axis=0, keepdims=True
    )


def layer_kernel(
    chips,
    n_t,
    heads,
    tok,
    cot,
    gain_attn,
    gain_ffn,
    w_query,
    w_key,
    w_value,
    w_output,
    w_in,
    w_out,
    table,
    router,
    routes,
    lengths,
    mixed_out,
    gtok_out,
    gain_attn_out,
    gain_ffn_out,
    query_out,
    key_out,
    value_out,
    output_out,
    bias_out,
    router_out,
    in_out,
    out_out,
    xg,
    cg,
    fg,
    bg,
    aw,
    ew,
    q3,
    k3,
    v3,
    att,
    probs,
    bias,
    seg_col,
    route_col,
    pick,
    slots,
    gslots,
    active,
    slope,
    gpre,
    eo,
    gcols,
    part_b,
    part_r,
    part_g,
    part_n,
    pass_buf,
    total,
    middle,
    gmid,
    gq3,
    gk3,
    gv3,
    gk_acc,
    gv_acc,
    diag,
    gexp,
    gexp_mate,
    gexp_chips,
    gatt,
    gatt_mate,
    gatt_chips,
    small,
    small_t,
    small_m,
    small_in,
    send_sem,
    recv_sem,
):
    bf, f32 = jnp.bfloat16, jnp.float32
    me, at = lax.axis_index("dp"), lax.axis_index("tensor")
    links = Links(send_sem, recv_sem)
    rows, width = tok.shape
    size = n_t * rows
    cap, tail = slots.shape[1], table.shape[0]
    chip, core = me // 2, me % 2
    mate = chip * 2 + 1 - core

    def chip_peer(k):
        return ((chip + k) % chips) * 2 + core

    barrier = pltpu.get_barrier_semaphore()
    for k in range(1, n_t):
        pl.semaphore_signal(
            barrier, 1, device_id={"tensor": (at + k) % n_t}, device_id_type=pl.DeviceIdType.MESH
        )
    for k in range(chips):
        pl.semaphore_signal(
            barrier,
            1,
            device_id={"dp": mate if k == 0 else chip_peer(k)},
            device_id_type=pl.DeviceIdType.MESH,
        )
    width = tok.shape[1]
    gain_a, gain_f = gain_attn[...].reshape(1, width), gain_ffn[...].reshape(1, width)
    x_own = tok[...].astype(f32)
    xg[at] = rms_scale(x_own, gain_a).astype(bf)
    cg[at] = cot[...]
    for i, own in enumerate((w_query, w_key, w_value, w_output)):
        aw[me, i] = own[...]
    for e in range(EXPERTS):
        ew[me, e] = w_in[e]
        ew[me, 2 + e] = w_out[e]
    pl.semaphore_wait(barrier, n_t - 1 + chips)

    x_step, x_end = line_gather(links, xg, at, n_t)
    c_step, c_end = line_gather(links, cg, at, n_t)
    f_step, f_end = line_gather(links, fg, at, n_t)
    b_step, b_end = line_gather(links, bg, at, n_t)
    attn_w = ChipGather(links, aw.at[me], aw, me, chips)
    exp_w = ChipGather(links, ew.at[me], ew, me, chips)
    x_step(0)
    attn_w.start()
    exp_w.start()

    lane = lax.broadcasted_iota(jnp.int32, (BUCKETS, 2 * size), 1)
    offset = jnp.where(lane < size, lane, lane - 2 * size)
    hit = (bucket_of(offset) == lax.broadcasted_iota(jnp.int32, (BUCKETS, 2 * size), 0)).astype(f32)
    every = jnp.dot(table[...], hit, precision=highest, preferred_element_type=f32)
    head_row = lax.broadcasted_iota(jnp.int32, every.shape, 0)
    for h in range(heads):
        by_offset = jnp.sum(
            jnp.where(head_row == at * heads + h, every, 0.0), axis=0, keepdims=True
        )
        for s in range(n_t):
            wide = jnp.broadcast_to(by_offset, (rows, 2 * size))
            bias[h, pl.ds(s * rows, rows)] = pltpu.roll(
                wide, s * rows, 1, stride=1, stride_axis=0
            )[:, :size]
    ends = [lengths[0, 0]]
    for s in range(1, lengths.shape[1]):
        ends.append(ends[-1] + lengths[0, s])

    def segments(position):
        seg = jnp.zeros(position.shape, jnp.int32)
        for end in ends:
            seg = seg + (position >= end).astype(jnp.int32)
        return seg

    seg_row = segments(lax.broadcasted_iota(jnp.int32, (1, size), 1))
    seg_col[...] = segments(lax.broadcasted_iota(jnp.int32, (size, 1), 0))
    x_step(1)
    turned = jnp.broadcast_to(routes[...].astype(f32), (128, size)).T
    route_col[...] = turned[:, 0:1]
    route = turned.astype(jnp.int32)
    onehot = route == lax.broadcasted_iota(jnp.int32, (size, 128), 1)
    lower = (
        lax.broadcasted_iota(jnp.int32, (size, size), 1)
        < lax.broadcasted_iota(jnp.int32, (size, size), 0)
    ).astype(f32).astype(bf)
    before = jnp.dot(lower, onehot.astype(f32).astype(bf), preferred_element_type=f32)
    place = jnp.sum(jnp.where(onehot, before, 0.0), axis=1, keepdims=True).astype(jnp.int32)
    place = place + route[:, 0:1] * cap
    pick[...] = (
        (place == lax.broadcasted_iota(jnp.int32, (size, EXPERTS * cap), 1)).astype(f32).astype(bf)
    )
    for k in range(2, n_t - 1):
        x_step(k)
    attn_w.forward()
    x_end()
    c_step(0)
    attn_w.finish()

    def attn_weight(i):
        return aw[:, i].reshape(width, heads * HEAD_DIM)

    @pl.loop(0, n_t)
    def _(s):
        for i, dest in enumerate((q3, k3, v3)):
            made = jnp.dot(xg[s], attn_weight(i), preferred_element_type=f32).astype(bf)
            for h in range(heads):
                dest[h, pl.ds(pl.multiple_of(s * rows, rows), rows)] = made[
                    :, h * HEAD_DIM : (h + 1) * HEAD_DIM
                ]

    c_step(1)

    @pl.loop(0, n_t)
    def _(s):
        here = pl.ds(pl.multiple_of(s * rows, rows), rows)
        same = seg_col[here] == seg_row
        for h in range(heads):
            scores = dot_nt(q3[h, here], k3[h]) + bias[h, here]
            scores = jnp.where(same, scores, -1e30)
            weights = jnp.exp(scores - jnp.max(scores, axis=-1, keepdims=True))
            p = weights * (1.0 / jnp.sum(weights, axis=-1, keepdims=True))
            probs[h, here] = p
            att[here, h * HEAD_DIM : (h + 1) * HEAD_DIM] = jnp.dot(
                p.astype(bf), v3[h], preferred_element_type=f32
            ).astype(bf)
        part_b[s] = dot_nt(att[here], attn_weight(3)).astype(bf)

    def scatter(i, part):
        return line_scatter(
            links, part, pass_buf.at[i, 0], pass_buf.at[i, 1], pass_buf.at[i, 2],
            pass_buf.at[i, 3], at, n_t,
        )

    br_step, br_end = scatter(0, part_b)
    gn_step, gn_end = scatter(1, part_g)
    re_step, re_end = scatter(2, part_r)
    at_step, at_end = scatter(3, part_n)
    for k in range(n_t - 1):
        br_step(k)
    for k in range(2, n_t - 1):
        c_step(k)
    br_end(total)
    middle[...] = tok[...].astype(f32) + total[...]
    fg[at] = rms_scale(middle[...], gain_f).astype(bf)
    f_step(0)
    c_end()
    exp_w.forward()
    for k in range(1, n_t - 1):
        f_step(k)
    f_end()

    def block(s):
        return pl.ds(pl.multiple_of(s * rows, rows), rows)

    @pl.loop(0, n_t)
    def _(s):
        values = fg[s].astype(f32)
        first = jnp.sum(values * router[0:1, :], axis=1, keepdims=True)
        second = jnp.sum(values * router[1:2, :], axis=1, keepdims=True)
        most = jnp.maximum(first, second)
        first, second = jnp.exp(first - most), jnp.exp(second - most)
        whole = 1.0 / (first + second)
        first, second = first * whole, second * whole
        is_second = route_col[block(s)]
        gate = jnp.where(is_second > 0.5, second, first)
        gcols[0, block(s)] = gate
        gcols[1, block(s)] = 1.0 - is_second - first
        gcols[2, block(s)] = is_second - second
        bg[s] = (cg[s].astype(f32) * gate).astype(bf)

    ffn_rows = fg[...].reshape(size, width)
    grad_rows = bg[...].reshape(size, width)
    for e in range(EXPERTS):
        chosen = pick[:, e * cap : (e + 1) * cap]
        slots[e] = dot_tn(chosen, ffn_rows).astype(bf)
        gslots[e] = dot_tn(chosen, grad_rows).astype(bf)
    exp_w.finish()
    cols = 256
    units = ew.shape[3]
    shard_rows = ew.shape[2]
    half = ew.shape[0] // 2
    wide_half = half * shard_rows

    def tile(j):
        return pl.ds(pl.multiple_of(j * cols, cols), cols)

    for e in range(EXPERTS):

        @pl.loop(0, units // cols)
        def _(j):
            pre = jnp.dot(
                slots[e], ew[:, e, :, tile(j)].reshape(width, cols), preferred_element_type=f32
            )
            value, rate = gelu_both(pre)
            active[e, :, tile(j)] = value.astype(bf)
            slope[e, :, tile(j)] = rate

    for e in range(EXPERTS):
        for j in range(2):
            eo[e, :, j * wide_half : (j + 1) * wide_half] = dot_nt(
                active[e], ew[j * half : (j + 1) * half, 2 + e].reshape(wide_half, units)
            ).astype(bf)

    @pl.loop(0, n_t)
    def _(s):
        back = jnp.dot(
            pick[block(s)], eo[...].reshape(EXPERTS * cap, width), preferred_element_type=f32
        )
        part_r[s] = back.astype(bf)
        gcols[3, block(s)] = (
            jnp.sum(cg[s].astype(f32) * back, axis=1, keepdims=True) * gcols[0, block(s)]
        )

    for e in range(EXPERTS):

        @pl.loop(0, units // cols)
        def _(j):
            grad_active = jnp.dot(
                gslots[e], ew[:, 2 + e, :, tile(j)].reshape(width, cols), preferred_element_type=f32
            )
            gpre[e, :, tile(j)] = (grad_active * slope[e, :, tile(j)]).astype(bf)

    for e in range(EXPERTS):
        for j in range(2):
            eo[e, :, j * wide_half : (j + 1) * wide_half] = dot_nt(
                gpre[e], ew[j * half : (j + 1) * half, e].reshape(wide_half, units)
            ).astype(bf)
    small[...] = jnp.zeros_like(small)

    @pl.loop(0, n_t)
    def _(s):
        back = jnp.dot(
            pick[block(s)], eo[...].reshape(EXPERTS * cap, width), preferred_element_type=f32
        )
        values = fg[s].astype(f32)
        for e in range(EXPERTS):
            grad_logit = gcols[3, block(s)] * gcols[1 + e, block(s)]
            back = back + grad_logit * router[e : e + 1, :]
            small[tail + 2 + e : tail + 3 + e, :] += jnp.sum(values * grad_logit, axis=0, keepdims=True)
        part_g[s] = back.astype(bf)

    exp_g = ChipScatter(links, gexp, gexp_mate, gexp_chips, me, chips)
    gn_step(0)

    def weight_grads(left, right, i):
        @pl.loop(0, units // cols)
        def _(j):
            gexp[:, i, :, tile(j)] = (
                dot_tn(left, right[:, tile(j)]).astype(bf).reshape(2 * half, shard_rows, cols)
            )

    for e in range(EXPERTS):
        weight_grads(slots[e], gpre.at[e], e)
    for k in range(1, n_t - 2):
        gn_step(k)
    for e in range(EXPERTS):
        weight_grads(gslots[e], active.at[e], 2 + e)
    for k in range(max(1, n_t - 2), n_t - 1):
        gn_step(k)
    exp_g.start()
    gn_end(total)
    norm_back, gain_part = rms_back(middle[...], gain_f, total[...])
    small[tail + 1 : tail + 2, :] = gain_part
    grad_mid = cot[...].astype(f32) + norm_back
    gmid[...] = grad_mid
    bg[at] = grad_mid.astype(bf)
    b_step(0)
    exp_g.middle()
    for k in range(1, n_t - 1):
        b_step(k)
    b_end()
    re_step(0)

    diag[...] = jnp.zeros_like(diag)
    gk_acc[...] = jnp.zeros_like(gk_acc)
    gv_acc[...] = jnp.zeros_like(gv_acc)
    mirror = (
        lax.broadcasted_iota(jnp.int32, (rows, rows), 0)
        + lax.broadcasted_iota(jnp.int32, (rows, rows), 1)
        == rows - 1
    ).astype(f32).astype(bf)

    def attn_back(s):
        here = block(s)
        same = seg_col[here] == seg_row
        grad_att = jnp.dot(bg[s], attn_weight(3), preferred_element_type=f32).astype(bf)
        for h in range(heads):
            g_part = grad_att[:, h * HEAD_DIM : (h + 1) * HEAD_DIM]
            p = probs[h, here]
            grad_p = dot_nt(g_part, v3[h])
            row_dot = jnp.sum(grad_p * p, axis=1, keepdims=True)
            grad_s = jnp.where(same, p * (grad_p - row_dot), 0.0).astype(bf)
            gv_acc[h] += dot_tn(p.astype(bf), g_part)
            gk_acc[h] += dot_tn(grad_s, q3[h, here])
            gq3[here, h * HEAD_DIM : (h + 1) * HEAD_DIM] = jnp.dot(
                grad_s, k3[h], preferred_element_type=f32
            ).astype(bf)
            turned = jnp.dot(mirror, grad_s, preferred_element_type=f32)
            turned = jnp.concatenate([turned, jnp.zeros((rows, rows), f32)], axis=1)
            turned = pltpu.roll(turned, 0, 1, stride=1, stride_axis=0)
            folded = jnp.sum(turned.reshape(rows // 8, 8, size + rows), axis=0)
            base = pl.multiple_of(size - rows - s * rows, rows)
            diag[h, :, pl.ds(base, size + rows)] += folded

    @pl.loop(0, n_t // 2)
    def _(s):
        attn_back(s)

    for k in range(1, n_t - 2):
        re_step(k)

    @pl.loop(n_t // 2, n_t)
    def _(s):
        attn_back(s)

    for h in range(heads):
        gk3[:, h * HEAD_DIM : (h + 1) * HEAD_DIM] = gk_acc[h].astype(bf)
        gv3[:, h * HEAD_DIM : (h + 1) * HEAD_DIM] = gv_acc[h].astype(bf)

    @pl.loop(0, n_t)
    def _(s):
        back = dot_nt(gq3[block(s)], attn_weight(0))
        back = back + dot_nt(gk3[block(s)], attn_weight(1))
        back = back + dot_nt(gv3[block(s)], attn_weight(2))
        part_n[s] = back.astype(bf)
        small[tail : tail + 1, :] += jnp.sum(back * xg[s].astype(f32), axis=0, keepdims=True)

    at_step(0)
    small[tail : tail + 1, :] = small[tail : tail + 1, :] / gain_a
    spot = lax.broadcasted_iota(jnp.int32, (2 * size, 128), 0) - (size - 1)
    fold = (bucket_of(spot) == lax.broadcasted_iota(jnp.int32, (2 * size, 128), 1)).astype(f32)
    line = lax.broadcasted_iota(jnp.int32, (small.shape[0], 128), 0)
    for h in range(heads):
        sums = jnp.dot(diag[h], fold, precision=highest, preferred_element_type=f32)
        sums = jnp.sum(sums, axis=0, keepdims=True)
        small[:, 0:128] += jnp.where(line == at * heads + h, sums, 0.0)

    first = links.take(n_t - 1)

    def small_line(k):
        return links.copy(first + k - 1, small, small_t.at[k - 1], {"tensor": (at + k) % n_t})

    for k in range(1, n_t):
        small_line(k).start()
    att_g = ChipScatter(links, gatt, gatt_mate, gatt_chips, me, chips)
    normed = xg[...].reshape(size, width)
    shape = (2 * half, shard_rows, heads * HEAD_DIM)
    gatt[:, 0] = dot_tn(normed, gq3[...]).astype(bf).reshape(shape)
    gatt[:, 1] = dot_tn(normed, gk3[...]).astype(bf).reshape(shape)
    for k in range(1, n_t - 2):
        at_step(k)
    gatt[:, 2] = dot_tn(normed, gv3[...]).astype(bf).reshape(shape)
    gatt[:, 3] = dot_tn(bg[...].reshape(size, width), att[...]).astype(bf).reshape(shape)
    att_g.start()
    for k in range(max(1, n_t - 2), n_t - 1):
        at_step(k)
    joined = small[...]
    for k in range(1, n_t):
        small_line(k).wait_recv()
        joined = joined + small_t[k - 1]
    small_m[0] = joined
    second = links.take(chips)
    swap = links.copy(second, small_m.at[0], small_in.at[0], {"dp": mate})
    swap.start()
    att_g.middle()
    swap.wait_recv()
    small_m[1] = small_m[0] + small_in[0]

    def small_chip(k):
        return links.copy(second + k, small_m.at[1], small_in.at[k], {"dp": chip_peer(k)})

    for k in range(1, chips):
        small_chip(k).start()
    for k in range(max(1, n_t - 2), n_t - 1):
        re_step(k)
    exp_g.finish([in_out.at[0], in_out.at[1], out_out.at[0], out_out.at[1]])
    at_end(total)
    tok_back, _ = rms_back(tok[...].astype(f32), gain_a, total[...])
    gtok_out[...] = gmid[...] + tok_back
    re_end(total)
    own_gate = gcols[0, block(at)]
    mixed_out[...] = (middle[...] + own_gate * total[...]).astype(bf)
    joined = small_m[1]
    for k in range(1, chips):
        small_chip(k).wait_recv()
        joined = joined + small_in[k]
    gain_attn_out[...] = joined[tail : tail + 1]
    gain_ffn_out[...] = joined[tail + 1 : tail + 2]
    router_out[...] = joined[tail + 2 : tail + 4]
    bias_out[...] = joined[0:tail, 0:BUCKETS]
    att_g.finish([query_out, key_out, value_out, output_out])
    for k in range(1, n_t):
        small_line(k).wait_send()
    swap.wait_send()
    for k in range(1, chips):
        small_chip(k).wait_send()


def hand_on(*refs):
    half = len(refs) // 2
    for source, dest in zip(refs[:half], refs[half:]):
        dest[...] = source[...]


def fused_layer(
    tokens, gain_attn, gain_ffn, w_query, w_key, w_value, w_output, bias_table, router,
    w_in, w_out, routes, lengths, cotangent,
):
    bf, f32 = jnp.bfloat16, jnp.float32
    n_dp, n_t = lax.axis_size("dp"), lax.axis_size("tensor")
    chips = n_dp // 2
    rows, width = tokens.shape
    size = rows * n_t
    cap = 3 * size // (2 * EXPERTS)
    shard, head_width = w_query.shape
    heads = head_width // HEAD_DIM
    units = w_in.shape[2]
    all_heads = bias_table.shape[1]
    small_rows = -(-(4 + all_heads) // 8) * 8
    vm = pl.BlockSpec(memory_space=pltpu.VMEM)
    V = pltpu.VMEM
    group = (n_t, rows, width)
    scratch = [
        V(group, bf), V(group, bf), V(group, bf), V(group, bf),
        V((n_dp, 4, shard, head_width), bf), V((n_dp, 4, shard, units), bf),
        V((heads, size, HEAD_DIM), bf), V((heads, size, HEAD_DIM), bf),
        V((heads, size, HEAD_DIM), bf),
        V((size, head_width), bf),
        V((heads, size, size), f32), V((heads, size, size), f32),
        V((size, 1), jnp.int32), V((size, 1), f32), V((size, EXPERTS * cap), bf),
        V((EXPERTS, cap, width), bf), V((EXPERTS, cap, width), bf),
        V((EXPERTS, cap, units), bf), V((EXPERTS, cap, units), f32), V((EXPERTS, cap, units), bf),
        V((EXPERTS, cap, width), bf), V((4, size, 1), f32),
        V(group, bf), V(group, bf), V(group, bf), V(group, bf),
        V((4, 4, n_t - 1, rows, width), bf),
        V((rows, width), f32), V((rows, width), f32), V((rows, width), f32),
        V((size, head_width), bf), V((size, head_width), bf), V((size, head_width), bf),
        V((heads, size, HEAD_DIM), f32), V((heads, size, HEAD_DIM), f32),
        V((heads, 8, 2 * size), f32),
        V((n_dp, 4, shard, units), bf), V((chips, 4, shard, units), bf),
        V((chips - 1, 4, shard, units), bf),
        V((n_dp, 4, shard, head_width), bf), V((chips, 4, shard, head_width), bf),
        V((chips - 1, 4, shard, head_width), bf),
        V((small_rows, width), f32), V((n_t - 1, small_rows, width), f32),
        V((2, small_rows, width), f32), V((chips, small_rows, width), f32),
        pltpu.SemaphoreType.DMA((256,)), pltpu.SemaphoreType.DMA((256,)),
    ]
    wide = jax.ShapeDtypeStruct((1, width), f32)
    square = jax.ShapeDtypeStruct((shard, head_width), f32)
    tall = jax.ShapeDtypeStruct((EXPERTS, shard, units), f32)
    made = pl.pallas_call(
        functools.partial(layer_kernel, chips, n_t, heads),
        out_shape=(
            jax.ShapeDtypeStruct((rows, width), bf),
            jax.ShapeDtypeStruct((rows, width), f32),
            wide, wide, square, square, square, square,
            jax.ShapeDtypeStruct(bias_table.shape[::-1], f32),
            jax.ShapeDtypeStruct((EXPERTS, width), f32),
            tall, tall,
        ),
        in_specs=[vm] * 13 + [pl.BlockSpec(memory_space=pltpu.SMEM)],
        out_specs=[vm] * 12,
        scratch_shapes=scratch,
        compiler_params=pltpu.CompilerParams(
            collective_id=0, has_side_effects=True, vmem_limit_bytes=60 * 1024 * 1024
        ),
    )(
        tokens, cotangent, gain_attn, gain_ffn,
        w_query, w_key, w_value, w_output, w_in.transpose(1, 0, 2), w_out.transpose(1, 0, 2),
        bias_table.T, router.T, routes.reshape(1, size), lengths,
    )
    made = pl.pallas_call(
        hand_on,
        out_shape=tuple(jax.ShapeDtypeStruct(one.shape, one.dtype) for one in made),
        in_specs=[vm] * 12,
        out_specs=[vm] * 12,
    )(*made)
    return (
        made[0], made[1], made[2][0], made[3][0], *made[4:8], made[8].T, made[9].T,
        made[10].transpose(1, 0, 2), made[11].transpose(1, 0, 2),
    )


def solution(mesh):
    in_specs = (
        P(("dp", "tensor"), None),
        P(),
        P(),
        P("dp", "tensor"),
        P("dp", "tensor"),
        P("dp", "tensor"),
        P("dp", "tensor"),
        P(),
        P(),
        P("dp", None, "tensor"),
        P("dp", None, "tensor"),
        P("dp", None),
        P("dp", None),
        P(("dp", "tensor"), None),
    )
    out_specs = (
        P(("dp", "tensor"), None),
        P(("dp", "tensor"), None),
        P(),
        P(),
        P("dp", "tensor"),
        P("dp", "tensor"),
        P("dp", "tensor"),
        P("dp", "tensor"),
        P(),
        P(),
        P("dp", None, "tensor"),
        P("dp", None, "tensor"),
    )

    def layer(*arrays):
        shard_rows, chips = arrays[3].shape[0], mesh.shape["dp"] // 2
        fits = shard_rows % 16 == 0 and mesh.shape["dp"] == 2 * chips and chips > 1
        return (fused_layer if fits else on_device)(*arrays)

    return jax.shard_map(
        layer, mesh=mesh, in_specs=in_specs, out_specs=out_specs, check_vma=False
    )
```
